256 devices in a mesh: grp: 4 (over y_hi, core), dp: 64 (over x, y_lo, z).
Axes of the slice: x: 4, y: 4 (y_hi: 2, y_lo: 2; y = y_hi * 2 + y_lo), z: 8, core: 2. Of those that a mesh axis runs over, the one named last changes fastest.
Arguments:
- normed: bfloat16 [32768, 704], P(('grp', 'dp')), may hold values from -6 to 6
- pre_gelu: bfloat16 [32768, 2816], P(('grp', 'dp')), may hold values from -45 to 45
- out_grad: bfloat16 [32768, 2816], P(('grp', 'dp')), may hold values from -24 to 24
- grn_gain: float32 [2816], replicated, may hold values from -4 to 4
Outputs:
- pre_grad: bfloat16 [32768, 2816], P(('grp', 'dp'))
- w_up_grad: float32 [2816, 704], P(('grp', 'dp'))
- gain_grad: float32 [2816], P(('grp', 'dp'))
- shift_grad: float32 [2816], P(('grp', 'dp'))
- bias_grad: float32 [2816], P(('grp', 'dp'))
The draws below stay inside these ranges and needn't reach their ends.
All inputs are finite; a program needn't handle non-finite values.
Results may differ from the reference program's by a relative error of at most 0.007.
Values sent between devices are 32-bit elements; how exact they have to be, the bound alone decides.
No kernel may reach another device: no remote copies, remote signals or barrier semaphores. Data moves between devices by JAX's collectives and lax.ppermute only.
A program may use at most 64 MiB of HBM per device.

```python
import math
import jax
import jax.numpy as jnp
from jax import lax

C = 704
H = 2816
IMG_TOK = 256
TOKENS = 32768
IMAGES = 128


def draw_pre_gelu(key, part):
    key = jax.random.fold_in(key, 7)
    base_key, row_key, col_key = jax.random.split(key, 3)
    base = jnp.clip(jax.random.normal(base_key, (TOKENS, H), jnp.float32), -5.0, 5.0)
    row_scale = jnp.exp(jax.random.uniform(row_key, (TOKENS, 1), jnp.float32, math.log(0.3), math.log(3.0)))
    col_scale = jnp.exp(jax.random.uniform(col_key, (1, H), jnp.float32, math.log(0.3), math.log(3.0)))
    return (base * row_scale * col_scale).astype(jnp.bfloat16)


def spiked(result, stream_key, source, target, parts, factor):
    owner, partner = [(jnp.arange(result.shape[dim]) // (result.shape[dim] // parts)).reshape([-1 if axis == dim else 1 for axis in range(result.ndim)]) for dim in (source, target)]
    chosen = jax.random.permutation(stream_key, parts)[partner]
    strong = (owner == chosen) | (owner == (partner + parts // 2) % parts)
    return jnp.where(strong, factor * result, result)


def steps_of(key, dims, pieces, low, largest):
    gain = 1.0
    for position, parts in pieces:
        steps = jax.random.uniform(jax.random.fold_in(jax.random.fold_in(key, 6), position), (parts,), jnp.float32, low / len(pieces), largest / len(pieces))
        gain = gain * jnp.repeat(jnp.exp(steps), dims[position] // parts).reshape((-1,) + (1,) * (len(dims) - 1 - position))
    return gain


def scatter_about(own_key, dims, scale, most, cuts=(), held_as=jnp.bfloat16):
    values = jax.random.normal(own_key, dims, jnp.float32) * scale
    if len(cuts) > 0:
        values = steps_of(own_key, dims, cuts, -0.22, 0.18) * values
    return jnp.clip(values, min=-most, max=most).astype(held_as)


def gaussian_with(rng, extent, scale, bound, cuts, heavy, held_as=jnp.bfloat16):
    result = scale * jax.random.normal(rng, extent, jnp.float32)
    if cuts:
        result = result * steps_of(rng, extent, cuts, -0.22, 0.18)
    return jnp.clip(spiked(result, jax.random.fold_in(rng, 3), *heavy), -bound, bound).astype(held_as)


def setup_inputs(seed: int = 0) -> dict:
    arg_keys = jax.random.split(jax.random.key(seed), 5)
    return {
        "normed": scatter_about(arg_keys[0], (TOKENS, C), 1.0, 6.0, ((0, 256),)),
        "pre_gelu": draw_pre_gelu(jax.random.fold_in(arg_keys[4], 71), 0),
        "out_grad": gaussian_with(arg_keys[2], (TOKENS, H), 1.0, 24.0, ((0, 256),), (0, 1, 256, 6.0)),
        "grn_gain": scatter_about(arg_keys[3], (H,), 1.0, 4.0, (), jnp.float32),
    }


root_half = 0.7071067811865476
inv_root_two_pi = 0.3989422804014327

def gelu_pair(pre_gelu):
    values = pre_gelu.astype(jnp.float32)
    cdf = 0.5 * (1.0 + jax.scipy.special.erf(values * root_half))
    gelu_out = values * cdf
    gelu_slope = cdf + values * jnp.exp(-0.5 * values * values) * inv_root_two_pi
    return (gelu_out, gelu_slope)

def image_grads(pre_gelu, out_grad, grn_gain):
    gelu_out, gelu_slope = gelu_pair(pre_gelu)
    upstream = out_grad.astype(jnp.float32)
    squares = lax.optimization_barrier(jnp.sum(gelu_out * gelu_out, axis=0))
    response = lax.optimization_barrier(jnp.sum(upstream * gelu_out, axis=0))
    channel_norm = jnp.sqrt(squares + 1e-06)
    norm_mean = jnp.mean(channel_norm) + 1e-06
    scaled = channel_norm / norm_mean
    scaled_grad = grn_gain * response
    units = channel_norm.shape[0]
    norm_grad = scaled_grad / norm_mean - jnp.sum(scaled_grad * channel_norm) / (units * norm_mean * norm_mean)
    act_grad = upstream * (grn_gain * scaled + 1.0) + gelu_out * (norm_grad / channel_norm)
    pre_grad = (act_grad * gelu_slope).astype(jnp.bfloat16)
    return (pre_grad, response * scaled, lax.optimization_barrier(jnp.sum(upstream, axis=0)), lax.optimization_barrier(jnp.sum(pre_grad.astype(jnp.float32), axis=0)))

def reference(normed, pre_gelu, out_grad, grn_gain):
    images = (normed.reshape(IMAGES, IMG_TOK, C), pre_gelu.reshape(IMAGES, IMG_TOK, H), out_grad.reshape(IMAGES, IMG_TOK, H))

    def one_image(carry, item):
        normed_img, pre_img, grad_img = item
        pre_grad, gain_term, shift_term, bias_term = image_grads(pre_img, grad_img, grn_gain)
        weight_sum = carry[0] + jnp.dot(pre_grad.T, normed_img, preferred_element_type=jnp.float32)
        return ((weight_sum, carry[1] + gain_term, carry[2] + shift_term, carry[3] + bias_term), pre_grad)
    zeros_unit = jnp.zeros((H,), jnp.float32)
    start_carry = (jnp.zeros((H, C), jnp.float32), zeros_unit, zeros_unit, zeros_unit)
    totals, pre_grads = lax.scan(one_image, start_carry, images)
    return (pre_grads.reshape(TOKENS, H), totals[0], totals[1], totals[2], totals[3])
```

```python
import jax
import jax.numpy as jnp
import numpy as np
from jax import lax
from jax.experimental import pallas as pl
from jax.experimental.pallas import tpu as pltpu
from jax.sharding import Mesh, PartitionSpec as P

root_half = 0.7071067811865476
inv_root_two_pi = 0.3989422804014327

AXES = ("yh", "core", "x", "yl", "z")
SIZES = (2, 2, 4, 2, 8)
ROWS = 128
C = 704
H = 2816
BLOCK = 88
OWN = 11
LANES = 128
MIB = 1 << 20


def pairs(target):
    found = []
    for i in range(256):
        yh, core, x, yl, z = (int(v) for v in np.unravel_index(i, SIZES))
        core2, x2, y2, z2 = target(core, x, 2 * yh + yl, z)
        place = (y2 // 2 % 2, core2 % 2, x2 % 4, y2 % 2, z2 % 8)
        found.append((i, int(np.ravel_multi_index(place, SIZES))))
    return found


def send(value, target):
    return lax.ppermute(value, AXES, pairs(target))


def other_core(core, x, y, z):
    return 1 - core, x, y, z


def other_half(core, x, y, z):
    return core, x, y, z ^ 1


def along(k):
    return lambda core, x, y, z: (core, x + k, y, z) if core == 0 else (core, x, y + k, z)


def across(k):
    return lambda core, x, y, z: (1, x, y + k, z) if core == 0 else (0, x + k, y, z)


def beside(k):
    return lambda core, x, y, z: (core, x, y + k, z) if core == 0 else (core, x + k, y, z)


def call(body, out_shape, scratch=(), flops=0, moved=0, limit=24):
    return pl.pallas_call(
        body,
        out_shape=out_shape,
        scratch_shapes=scratch,
        compiler_params=pltpu.CompilerParams(vmem_limit_bytes=limit * MIB),
        cost_estimate=pl.CostEstimate(flops=flops, bytes_accessed=moved, transcendentals=0),
    )


def f32(*shape):
    return jax.ShapeDtypeStruct(shape, jnp.float32)


def widen(normed, wide):
    for k in range(5):
        wide[k * ROWS : (k + 1) * ROWS, :] = normed[:, k * LANES : (k + 1) * LANES].astype(jnp.float32)
    last = normed[:, 5 * LANES : C].astype(jnp.float32)
    wide[5 * ROWS : C, :] = jnp.concatenate([last[: ROWS // 2], last[ROWS // 2 :]], axis=1)


def narrow(*refs):
    *wides, out = refs
    lane = lax.broadcasted_iota(jnp.int32, (ROWS, LANES - 64), 1)
    ones = jnp.where(lane == 0, 1.0, 0.0)
    for s, wide in enumerate(wides):
        rows = slice(s * ROWS, (s + 1) * ROWS)
        for k in range(5):
            out[rows, k * LANES : (k + 1) * LANES] = wide[k * ROWS : (k + 1) * ROWS, :].astype(jnp.bfloat16)
        last = wide[5 * ROWS : C, :]
        both = jnp.concatenate([last[:, :64], last[:, 64:]], axis=0)
        out[rows, 5 * LANES :] = jnp.concatenate([both, ones], axis=1).astype(jnp.bfloat16)


def statistics(pre_gelu, out_grad, sums, shift, gelu, slope):
    for k in range(H // LANES):
        cols = slice(k * LANES, (k + 1) * LANES)
        values = pre_gelu[:, cols].astype(jnp.float32)
        upstream = out_grad[:, cols].astype(jnp.float32)
        cdf = 0.5 * (1.0 + lax.erf(values * root_half))
        gelu_out = values * cdf
        gelu[:, cols] = gelu_out
        slope[:, cols] = cdf + values * jnp.exp(-0.5 * values * values) * inv_root_two_pi
        sums[0:1, cols] = jnp.sum(gelu_out * gelu_out, axis=0, keepdims=True)
        sums[1:2, cols] = jnp.sum(upstream * gelu_out, axis=0, keepdims=True)
        shift[0:1, cols] = jnp.sum(upstream, axis=0, keepdims=True)


def gradient(sums, other, shift, gain, out_grad, gelu, slope, pre_grad, *rest):
    chunks, (turned, gains, shifts) = rest[:8], rest[8:]
    squares = sums[0:1, :] + other[0:1, :]
    response = sums[1:2, :] + other[1:2, :]
    channel_norm = jnp.sqrt(squares + 1e-06)
    norm_mean = jnp.sum(channel_norm, axis=1, keepdims=True) * (1.0 / H) + 1e-06
    scaled = channel_norm / norm_mean
    scaled_grad = gain[...] * response
    norm_grad = scaled_grad / norm_mean - jnp.sum(scaled_grad * channel_norm, axis=1, keepdims=True) / (
        H * norm_mean * norm_mean
    )
    of_upstream = gain[...] * scaled + 1.0
    of_gelu = norm_grad / channel_norm
    gain_term = sums[1:2, :] * scaled
    shift_term = shift[...]
    for k in range(H // LANES):
        cols = slice(k * LANES, (k + 1) * LANES)
        upstream = out_grad[:, cols].astype(jnp.float32)
        act_grad = upstream * of_upstream[:, cols] + gelu[:, cols] * of_gelu[:, cols]
        rounded = (act_grad * slope[:, cols]).astype(jnp.bfloat16)
        pre_grad[:, cols] = rounded
        turned[cols, :] = rounded.astype(jnp.float32).T
    both = jnp.concatenate([gain_term, shift_term, jnp.zeros((6, H), jnp.float32)], axis=0)
    for b in range(H // BLOCK):
        tile, start = divmod(b * BLOCK, LANES)
        window = both[:, tile * LANES : min((tile + 2) * LANES, H)]
        if start:
            window = pltpu.roll(window, window.shape[1] - start, 1)
        gains[b : b + 1, :] = window[0:1, :LANES]
        shifts[b : b + 1, :] = window[1:2, :LANES]
    core, x = lax.axis_index("core"), lax.axis_index("x")
    y = 2 * lax.axis_index("yh") + lax.axis_index("yl")
    for of_other in range(2):
        to = core if of_other == 0 else 1 - core
        mine, beside_mine = jnp.where(to == 0, x, y), jnp.where(to == 0, y, x)
        for j in range(4):
            chunk = chunks[of_other * 4 + j]
            d = lax.rem(mine + j, 4)
            for i in range(4):
                e = lax.rem(beside_mine + i, 4)
                block_x, block_y = jnp.where(to == 0, d, e), jnp.where(to == 0, e, d)
                b = (block_y // 2) * 16 + to * 8 + block_x * 2 + lax.rem(block_y, 2)
                start = pl.multiple_of(b * BLOCK, 8)
                chunk[i * BLOCK : (i + 1) * BLOCK, :] = turned[pl.ds(start, BLOCK), :]
                chunk[4 * BLOCK + i : 4 * BLOCK + i + 1, :] = gains[pl.ds(b, 1), :]
                chunk[4 * BLOCK + 4 + i : 4 * BLOCK + 5 + i, :] = shifts[pl.ds(b, 1), :]


def product(*refs):
    parts, right, outs, left = refs[:8], refs[8], refs[9:13], refs[13]
    for s, part in enumerate(parts):
        left[:, s * ROWS : (s + 1) * ROWS] = part[: 4 * BLOCK, :].astype(jnp.bfloat16)
    small = parts[0][4 * BLOCK :, :]
    for part in parts[1:]:
        small = small + part[4 * BLOCK :, :]
    small = small.T
    lane = lax.broadcasted_iota(jnp.int32, (BLOCK, LANES), 1)
    for k in range(3):
        cols = slice(2 * k * LANES, 2 * (k + 1) * LANES)
        total = jnp.dot(left[...], right[:, cols], preferred_element_type=jnp.float32)
        for i, out in enumerate(outs):
            rows = total[i * BLOCK : (i + 1) * BLOCK, :]
            if k < 2:
                out[:, cols] = rows
            else:
                out[:, 4 * LANES : 5 * LANES] = rows[:, :LANES]
                last = rows[:, LANES:]
                last = jnp.where(lane == 65, small[:BLOCK, i : i + 1], last)
                last = jnp.where(lane == 66, small[:BLOCK, 4 + i : 5 + i], last)
                out[:, 5 * LANES :] = last


PACKED = 72


def gather_rows(a, b, c, d, out):
    for k in range(6):
        cols = slice(k * LANES, (k + 1) * LANES)
        total = (a[:, cols] + b[:, cols]) + (c[:, cols] + d[:, cols])
        for z in range(8):
            out[z, k * OWN : (k + 1) * OWN, :] = total[z * OWN : (z + 1) * OWN, :]
    out[:, 6 * OWN :, :] = jnp.zeros((8, PACKED - 6 * OWN, LANES), jnp.float32)


def finish(parts, weight, gain, shift, bias):
    total = parts[0]
    for z in range(1, 8):
        total = total + parts[z]
    for k in range(6):
        rows = total[k * OWN : (k + 1) * OWN, :]
        if k < 5:
            weight[:, k * LANES : (k + 1) * LANES] = rows
        else:
            weight[:, 5 * LANES :] = rows[:, :64]
            turned = jnp.concatenate([rows, jnp.zeros((5, LANES), jnp.float32)], axis=0).T
            bias[...] = turned[64:65, :OWN]
            gain[...] = turned[65:66, :OWN]
            shift[...] = turned[66:67, :OWN]


def on_device(normed, pre_gelu, out_grad, grn_gain):
    wide = call(widen, f32(C, LANES), moved=540_000)(normed)
    sums, shift, gelu, slope = call(
        statistics,
        [f32(2, H), f32(1, H), f32(ROWS, H), f32(ROWS, H)],
        flops=60 * ROWS * H,
        moved=4_400_000,
    )(pre_gelu, out_grad)
    other = send(sums, other_half)

    near = send(wide, other_core)
    from_below = send(wide, along(1))
    from_above = send(wide, along(-1))
    below_across = send(wide, across(1))
    above_across = send(wide, across(-1))
    far = send(from_below, along(1))
    far_across = send(above_across, along(-1))
    right = call(narrow, jax.ShapeDtypeStruct((8 * ROWS, 6 * LANES), jnp.bfloat16), moved=4_400_000)(
        wide, near, from_below, below_across, from_above, above_across, far, far_across
    )

    pre_grad, *chunks = call(
        gradient,
        [jax.ShapeDtypeStruct((ROWS, H), jnp.bfloat16)] + [f32(4 * BLOCK + 8, LANES)] * 8,
        scratch=[
            pltpu.VMEM((H, LANES), jnp.float32),
            pltpu.VMEM((H // BLOCK, LANES), jnp.float32),
            pltpu.VMEM((H // BLOCK, LANES), jnp.float32),
        ],
        flops=30 * ROWS * H,
        moved=6_000_000,
    )(sums, other, shift, grn_gain.reshape(1, H), out_grad, gelu, slope)
    keep, cross = chunks[:4], chunks[4:]
    parts = [
        keep[0],
        send(cross[0], other_core),
        send(keep[1], along(1)),
        send(cross[1], across(1)),
        send(keep[3], along(-1)),
        send(cross[3], across(-1)),
        send(keep[2], along(2)),
        send(cross[2], across(2)),
    ]
    own, *away = call(
        product,
        [f32(BLOCK, 6 * LANES)] * 4,
        scratch=[pltpu.VMEM((4 * BLOCK, 8 * ROWS), jnp.bfloat16)],
        flops=2 * 352 * 1024 * 768,
        moved=4_000_000,
    )(*parts, right)
    stage = [send(away[0], beside(1)), send(away[2], beside(-1)), send(away[1], beside(2))]
    rows = call(gather_rows, f32(8, PACKED, LANES), moved=1_400_000)(own, *stage)
    rows = lax.all_to_all(rows, "z", 0, 0, tiled=True)
    weight, gain, shift, bias = call(
        finish, [f32(OWN, C), f32(1, OWN), f32(1, OWN), f32(1, OWN)], moved=330_000
    )(rows)
    return pre_grad, weight, gain.reshape(OWN), shift.reshape(OWN), bias.reshape(OWN)


def solution(mesh):
    split = Mesh(mesh.devices.reshape(SIZES), AXES)
    return jax.shard_map(
        on_device,
        mesh=split,
        in_specs=(P(AXES, None), P(AXES, None), P(AXES, None), P()),
        out_specs=(P(AXES, None), P(AXES, None), P(AXES), P(AXES), P(AXES)),
        check_vma=False,
    )
```

```python
import jax
import jax.numpy as jnp
import numpy as np
from jax import lax
from jax.experimental import pallas as pl
from jax.experimental.pallas import tpu as pltpu
from jax.sharding import Mesh, PartitionSpec as P

root_half = 0.7071067811865476
inv_root_two_pi = 0.3989422804014327

AXES = ("yh", "core", "x", "yl", "z")
SIZES = (2, 2, 4, 2, 8)
ROWS = 128
C = 704
H = 2816
BLOCK = 88
OWN = 11
PART = 4 * BLOCK + 8
LANES = 128
MIB = 1 << 20
GUIDE = 20_000_000_000


def pairs(target):
    found = []
    for i in range(256):
        yh, core, x, yl, z = (int(v) for v in np.unravel_index(i, SIZES))
        core2, x2, y2, z2 = target(core, x, 2 * yh + yl, z)
        place = (y2 // 2 % 2, core2 % 2, x2 % 4, y2 % 2, z2 % 8)
        found.append((i, int(np.ravel_multi_index(place, SIZES))))
    return found


def send(value, target):
    return lax.ppermute(value, AXES, pairs(target))


def other_core(core, x, y, z):
    return 1 - core, x, y, z


def other_half(core, x, y, z):
    return core, x, y, z ^ 1


def along(k):
    return lambda core, x, y, z: (core, x + k, y, z) if core == 0 else (core, x, y + k, z)


def across(k):
    return lambda core, x, y, z: (1, x, y + k, z) if core == 0 else (0, x + k, y, z)


def beside(k):
    return lambda core, x, y, z: (core, x, y + k, z) if core == 0 else (core, x + k, y, z)


def call(body, out_shape, scratch=(), flops=0, moved=0, limit=24, **specs):
    return pl.pallas_call(
        body,
        out_shape=out_shape,
        **specs,
        scratch_shapes=scratch,
        compiler_params=pltpu.CompilerParams(vmem_limit_bytes=limit * MIB),
        cost_estimate=pl.CostEstimate(flops=flops, bytes_accessed=moved, transcendentals=0),
    )


def f32(*shape):
    return jax.ShapeDtypeStruct(shape, jnp.float32)


def narrow(*refs):
    *wides, out = refs
    for s, wide in enumerate(wides):
        top = wide.shape[0] - C
        out[:, s * ROWS : (s + 1) * ROWS] = wide[top:, :].astype(jnp.bfloat16)


CUTS = (0, 6, 12, 17, 22)


def statistics(
    normed_hbm, pre_gelu_hbm, out_grad_hbm, wide, sums, shift, gelu, slope, out_grad, pre_gelu, normed, sems, normed_sem
):
    copies = []
    for p, (start, stop) in enumerate(zip(CUTS[:-1], CUTS[1:])):
        cols = pl.ds(start * LANES, (stop - start) * LANES)
        for n, (source, target) in enumerate(((pre_gelu_hbm, pre_gelu), (out_grad_hbm, out_grad))):
            copies.append(pltpu.make_async_copy(source.at[:, cols], target.at[:, cols], sems.at[n, p]))
            copies[-1].start()
    last = pltpu.make_async_copy(normed_hbm, normed, normed_sem)
    last.start()
    for p, (start, stop) in enumerate(zip(CUTS[:-1], CUTS[1:])):
        copies[2 * p].wait()
        copies[2 * p + 1].wait()
        for k in range(start, stop):
            cols = slice(k * LANES, (k + 1) * LANES)
            values = pre_gelu[:, cols].astype(jnp.float32)
            upstream = out_grad[:, cols].astype(jnp.float32)
            cdf = 0.5 * (1.0 + lax.erf(values * root_half))
            gelu_out = values * cdf
            gelu[:, cols] = gelu_out
            slope[:, cols] = cdf + values * jnp.exp(-0.5 * values * values) * inv_root_two_pi
            sums[0:1, cols] = jnp.sum(gelu_out * gelu_out, axis=0, keepdims=True)
            sums[1:2, cols] = jnp.sum(upstream * gelu_out, axis=0, keepdims=True)
            shift[0:1, cols] = jnp.sum(upstream, axis=0, keepdims=True)
    last.wait()
    wide[...] = normed[...].astype(jnp.float32)


def gradient(sums, other, shift, gain, out_grad, gelu, slope, wide, result, keep, cross, *scratch):
    pre_grad, turned, gains, shifts, sems = scratch
    squares = sums[0:1, :] + other[0:1, :]
    response = sums[1:2, :] + other[1:2, :]
    channel_norm = jnp.sqrt(squares + 1e-06)
    norm_mean = jnp.sum(channel_norm, axis=1, keepdims=True) * (1.0 / H) + 1e-06
    scaled = channel_norm / norm_mean
    scaled_grad = gain[...] * response
    norm_grad = scaled_grad / norm_mean - jnp.sum(scaled_grad * channel_norm, axis=1, keepdims=True) / (
        H * norm_mean * norm_mean
    )
    of_upstream = gain[...] * scaled + 1.0
    of_gelu = norm_grad / channel_norm
    gain_term = sums[1:2, :] * scaled
    shift_term = shift[...]
    copies = []
    for p, (start, stop) in enumerate(zip(CUTS[:-1], CUTS[1:])):
        for k in range(start, stop):
            cols = slice(k * LANES, (k + 1) * LANES)
            upstream = out_grad[:, cols].astype(jnp.float32)
            act_grad = upstream * of_upstream[:, cols] + gelu[:, cols] * of_gelu[:, cols]
            rounded = (act_grad * slope[:, cols]).astype(jnp.bfloat16)
            pre_grad[:, cols] = rounded
            turned[cols, :] = rounded.astype(jnp.float32).T
        cols = pl.ds(start * LANES, (stop - start) * LANES)
        copies.append(pltpu.make_async_copy(pre_grad.at[:, cols], result.at[:, cols], sems.at[p]))
        copies[-1].start()
    both = jnp.concatenate([gain_term, shift_term, jnp.zeros((6, H), jnp.float32)], axis=0)
    for b in range(H // BLOCK):
        tile, start = divmod(b * BLOCK, LANES)
        window = both[:, tile * LANES : min((tile + 2) * LANES, H)]
        if start:
            window = pltpu.roll(window, window.shape[1] - start, 1)
        gains[b : b + 1, :] = window[0:1, :LANES]
        shifts[b : b + 1, :] = window[1:2, :LANES]
    core, x = lax.axis_index("core"), lax.axis_index("x")
    y = 2 * lax.axis_index("yh") + lax.axis_index("yl")
    for of_other in range(2):
        to = core if of_other == 0 else 1 - core
        mine, beside_mine = jnp.where(to == 0, x, y), jnp.where(to == 0, y, x)
        for j in range(4):
            chunk, top = (cross if of_other else keep), j * PART
            d = lax.rem(mine + j, 4)
            for i in range(4):
                e = lax.rem(beside_mine + i, 4)
                block_x, block_y = jnp.where(to == 0, d, e), jnp.where(to == 0, e, d)
                b = (block_y // 2) * 16 + to * 8 + block_x * 2 + lax.rem(block_y, 2)
                start = pl.multiple_of(b * BLOCK, 8)
                chunk[top + i * BLOCK : top + (i + 1) * BLOCK, :] = turned[pl.ds(start, BLOCK), :]
                row = top + 4 * BLOCK + i
                chunk[row : row + 1, :] = gains[pl.ds(b, 1), :]
                chunk[row + 4 : row + 5, :] = shifts[pl.ds(b, 1), :]
    cross[4 * PART :, :] = wide[...]
    for copy in copies:
        copy.wait()


def merge(keep, arrived, *outs):
    for j, out in enumerate(outs):
        out[:PART, :] = keep[j * PART : (j + 1) * PART, :]
        out[PART:, :] = arrived[j * PART : (j + 1) * PART, :]


def product(here, above, below, opposite, right_first, right_second, right_rest, *rest):
    outs, (left_first, left_second, left_rest) = rest[:4], rest[4:]
    one, two = slice(0, 4 * BLOCK), slice(PART, PART + 4 * BLOCK)
    sources = (
        (left_first, (here[one, :], below[one, :])),
        (left_second, (above[two, :], above[one, :], below[two, :])),
        (left_rest, (here[two, :], opposite[one, :], opposite[two, :])),
    )
    for left, values in sources:
        for s, value in enumerate(values):
            left[:, s * ROWS : (s + 1) * ROWS] = value.astype(jnp.bfloat16)
    rights = (right_first, right_second, right_rest)
    across_pixels = (((1,), (1,)), ((), ()))
    small = jnp.zeros((8, LANES), jnp.float32)
    for pair in (here, above, below, opposite):
        small = small + (pair[4 * BLOCK : PART, :] + pair[PART + 4 * BLOCK :, :])
    bias = 0.0
    for left, _ in sources:
        ones = jnp.ones((8, left.shape[1]), jnp.bfloat16)
        bias = bias + lax.dot_general(ones, left[...], across_pixels, preferred_element_type=jnp.float32)
    bias = jnp.concatenate([bias, jnp.zeros((8, 4 * LANES - 4 * BLOCK), jnp.float32)], axis=1)
    rows = []
    for i in range(4):
        tile, start = divmod(i * BLOCK, LANES)
        window = bias[:, tile * LANES : (tile + 2) * LANES]
        rows.append((pltpu.roll(window, 2 * LANES - start, 1) if start else window)[0:1, :LANES])
    small = jnp.concatenate([small, *rows, *rows], axis=0)
    for z in range(8):
        turned = pltpu.roll(small, LANES - z * OWN, 1) if z else small
        for i, out in enumerate(outs):
            row = z * PACKED + 61
            out[row : row + 1, :] = turned[8 + i : 9 + i, :]
            out[row + 1 : row + 2, :] = turned[i : i + 1, :]
            out[row + 2 : row + 3, :] = turned[4 + i : 5 + i, :]
    for group in range(3):
        cols = slice(2 * group * LANES, min(2 * (group + 1) * LANES, C))
        total = 0.0
        for (left, _), right in zip(sources, rights):
            total = total + lax.dot_general(
                left[...], right[cols, :], across_pixels, preferred_element_type=jnp.float32
            )
        if group == 2:
            last = total[:, LANES:]
            last = jnp.concatenate([last, last], axis=1)
            last = jnp.concatenate([last, jnp.zeros((8, LANES), jnp.float32)], axis=0)
            left_half = lax.broadcasted_iota(jnp.int32, (6, LANES), 1) < 64
        for i, out in enumerate(outs):
            for z in range(8):
                unit = i * BLOCK + z * OWN
                for k in range(2 * group, min(2 * group + 2, 5)):
                    row, col = z * PACKED + k * OWN, (k - 2 * group) * LANES
                    out[row : row + OWN, :] = total[unit : unit + OWN, col : col + LANES]
                if group == 2:
                    row = z * PACKED + 5 * OWN
                    out[row : row + 6, :] = jnp.where(left_half, last[unit : unit + 6], last[unit + 6 : unit + 12])


PACKED = 64


def add(a, b, c, d, out):
    out[...] = (a[...] + b[...]) + (c[...] + d[...])


def finish(parts, weight, gain, shift, bias):
    total = parts[0]
    for z in range(1, 8):
        total = total + parts[z]
    for k in range(5):
        weight[:, k * LANES : (k + 1) * LANES] = total[k * OWN : (k + 1) * OWN, :]
    last = total[5 * OWN : 5 * OWN + 6, :]
    weight[:6, 5 * LANES :] = last[:, :64]
    weight[6:, 5 * LANES :] = last[:5, 64:]
    bias[...] = total[61:62, :OWN]
    gain[...] = total[62:63, :OWN]
    shift[...] = total[63:64, :OWN]


def on_device(normed, pre_gelu, out_grad, grn_gain):
    bf16 = jnp.bfloat16
    wide, sums, shift, gelu, slope, upstream = call(
        statistics,
        [f32(C, ROWS), f32(2, H), f32(1, H), f32(ROWS, H), f32(ROWS, H), jax.ShapeDtypeStruct((ROWS, H), bf16)],
        scratch=[
            pltpu.VMEM((ROWS, H), bf16),
            pltpu.VMEM((C, ROWS), bf16),
            pltpu.SemaphoreType.DMA((2, 4)),
            pltpu.SemaphoreType.DMA,
        ],
        flops=60 * ROWS * H,
        moved=4_400_000,
        in_specs=[pl.BlockSpec(memory_space=pl.ANY)] * 3,
    )(*(pltpu.with_memory_space_constraint(v, pltpu.HBM) for v in (normed.T, pre_gelu, out_grad)))
    other = send(sums, other_half)

    from_below = send(wide, along(1))
    from_above = send(wide, along(-1))
    below_across = send(wide, across(1))
    above_across = send(wide, across(-1))

    def right_of(*wides, flops=GUIDE):
        shape = jax.ShapeDtypeStruct((C, len(wides) * ROWS), bf16)
        return call(narrow, shape, flops=flops, moved=4_400_000)(*wides)

    pre_grad, keep, cross = call(
        gradient,
        [jax.ShapeDtypeStruct((ROWS, H), bf16), f32(4 * PART, LANES), f32(4 * PART + C, LANES)],
        out_specs=[pl.BlockSpec(memory_space=pl.ANY)] + [pl.BlockSpec(memory_space=pltpu.VMEM)] * 2,
        scratch=[
            pltpu.VMEM((ROWS, H), bf16),
            pltpu.VMEM((H, LANES), jnp.float32),
            pltpu.VMEM((H // BLOCK, LANES), jnp.float32),
            pltpu.VMEM((H // BLOCK, LANES), jnp.float32),
            pltpu.SemaphoreType.DMA((4,)),
        ],
        flops=GUIDE // 5,
        moved=6_000_000,
    )(sums, other, shift, grn_gain.reshape(1, H), upstream, gelu, slope, wide)
    arrived = send(cross, other_core)
    right_first = right_of(wide, from_above, flops=GUIDE)
    arrived, right_first = lax.optimization_barrier((arrived, right_first))
    here, next_one, next_two, next_three = call(merge, [f32(2 * PART, LANES)] * 4, moved=4_400_000)(keep, arrived)
    far = send(from_below, along(1))
    far_across = send(above_across, along(-1))
    next_one, below_across, from_below = lax.optimization_barrier((next_one, below_across, from_below))
    right_second = right_of(below_across, from_below, above_across, flops=GUIDE)
    right_rest = right_of(arrived, far, far_across, flops=GUIDE)
    above = send(next_one, along(1))
    below = send(next_three, along(-1))
    opposite = send(next_two, along(2))
    own, *away = call(
        product,
        [f32(8 * PACKED, LANES)] * 4,
        scratch=[pltpu.VMEM((4 * BLOCK, n * ROWS), bf16) for n in (2, 3, 3)],
        flops=2 * 352 * 1024 * 768,
        moved=4_000_000,
    )(here, above, below, opposite, right_first, right_second, right_rest)
    stage = [send(away[1], beside(2)), send(away[0], beside(1)), send(away[2], beside(-1))]
    rows = call(add, f32(8 * PACKED, LANES), moved=1_400_000)(own, *stage)
    rows = lax.all_to_all(rows.reshape(8, PACKED, LANES), "z", 0, 0, tiled=True)
    weight, gain, shift, bias = call(
        finish, [f32(OWN, C), f32(1, OWN), f32(1, OWN), f32(1, OWN)], moved=330_000
    )(rows)
    return pre_grad, weight, gain.reshape(OWN), shift.reshape(OWN), bias.reshape(OWN)


def solution(mesh):
    split = Mesh(mesh.devices.reshape(SIZES), AXES)
    return jax.shard_map(
        on_device,
        mesh=split,
        in_specs=(P(AXES, None), P(AXES, None), P(AXES, None), P()),
        out_specs=(P(AXES, None), P(AXES, None), P(AXES), P(AXES), P(AXES)),
        check_vma=False,
    )
```

```python
import functools

import jax
import jax.numpy as jnp
import numpy as np
from jax import lax
from jax.experimental import pallas as pl
from jax.experimental.pallas import tpu as pltpu
from jax.sharding import Mesh, PartitionSpec as P

root_half = 0.7071067811865476
inv_root_two_pi = 0.3989422804014327

AXES = ("yh", "core", "x", "yl", "z")
SIZES = (2, 2, 4, 2, 8)
ROWS = 128
C = 704
H = 2816
BLOCK = 88
OWN = 11
HALF = BLOCK // 2
FIRST = 4 * HALF + 8
SECOND = 4 * HALF
PART = FIRST + SECOND
LANES = 128
MIB = 1 << 20
GUIDE = 20_000_000_000


def pairs(target):
    found = []
    for i in range(256):
        yh, core, x, yl, z = (int(v) for v in np.unravel_index(i, SIZES))
        core2, x2, y2, z2 = target(core, x, 2 * yh + yl, z)
        place = (y2 // 2 % 2, core2 % 2, x2 % 4, y2 % 2, z2 % 8)
        found.append((i, int(np.ravel_multi_index(place, SIZES))))
    return found


def send(value, target):
    return lax.ppermute(value, AXES, pairs(target))


def other_core(core, x, y, z):
    return 1 - core, x, y, z


def other_half(core, x, y, z):
    return core, x, y, z ^ 1


def along(k):
    return lambda core, x, y, z: (core, x + k, y, z) if core == 0 else (core, x, y + k, z)


def across(k):
    return lambda core, x, y, z: (1, x, y + k, z) if core == 0 else (0, x + k, y, z)


def beside(k):
    return lambda core, x, y, z: (core, x, y + k, z) if core == 0 else (core, x + k, y, z)


def call(body, out_shape, scratch=(), flops=0, moved=0, limit=24, **specs):
    return pl.pallas_call(
        body,
        out_shape=out_shape,
        **specs,
        scratch_shapes=scratch,
        compiler_params=pltpu.CompilerParams(vmem_limit_bytes=limit * MIB),
        cost_estimate=pl.CostEstimate(flops=flops, bytes_accessed=moved, transcendentals=0),
    )


def f32(*shape):
    return jax.ShapeDtypeStruct(shape, jnp.float32)


def narrow(*refs):
    *wides, out = refs
    for s, wide in enumerate(wides):
        top = wide.shape[0] - C
        out[:, s * ROWS : (s + 1) * ROWS] = wide[top:, :].astype(jnp.bfloat16)


CUTS = (0, 6, 12, 17, 22)


def widen(normed_hbm, wide, normed, sems):
    half = C // 2
    copies = [
        pltpu.make_async_copy(normed_hbm.at[pl.ds(p * half, half)], normed.at[pl.ds(p * half, half)], sems.at[p])
        for p in range(2)
    ]
    for copy in copies:
        copy.start()
    for p, copy in enumerate(copies):
        copy.wait()
        rows = slice(p * half, (p + 1) * half)
        wide[rows, :] = normed[rows, :].astype(jnp.float32)


def statistics(pre_gelu_hbm, out_grad_hbm, sums, shift, gelu, slope, out_grad, pre_gelu, sems):
    copies = []
    for p, (start, stop) in enumerate(zip(CUTS[:-1], CUTS[1:])):
        cols = pl.ds(start * LANES, (stop - start) * LANES)
        for n, (source, target) in enumerate(((pre_gelu_hbm, pre_gelu), (out_grad_hbm, out_grad))):
            copies.append(pltpu.make_async_copy(source.at[:, cols], target.at[:, cols], sems.at[n, p]))
            copies[-1].start()
    for p, (start, stop) in enumerate(zip(CUTS[:-1], CUTS[1:])):
        copies[2 * p].wait()
        copies[2 * p + 1].wait()
        for k in range(start, stop):
            cols = slice(k * LANES, (k + 1) * LANES)
            values = pre_gelu[:, cols].astype(jnp.float32)
            upstream = out_grad[:, cols].astype(jnp.float32)
            cdf = 0.5 * (1.0 + lax.erf(values * root_half))
            gelu_out = values * cdf
            gelu[:, cols] = gelu_out
            slope[:, cols] = cdf + values * jnp.exp(-0.5 * values * values) * inv_root_two_pi
            sums[0:1, cols] = jnp.sum(gelu_out * gelu_out, axis=0, keepdims=True)
            sums[1:2, cols] = jnp.sum(upstream * gelu_out, axis=0, keepdims=True)
            shift[0:1, cols] = jnp.sum(upstream, axis=0, keepdims=True)


def gradient(sums, other, shift, gain, out_grad, gelu, slope, wide, result, keep, cross, *scratch):
    pre_grad, turned, gains, shifts, sems = scratch
    squares = sums[0:1, :] + other[0:1, :]
    response = sums[1:2, :] + other[1:2, :]
    channel_norm = jnp.sqrt(squares + 1e-06)
    norm_mean = jnp.sum(channel_norm, axis=1, keepdims=True) * (1.0 / H) + 1e-06
    scaled = channel_norm / norm_mean
    scaled_grad = gain[...] * response
    norm_grad = scaled_grad / norm_mean - jnp.sum(scaled_grad * channel_norm, axis=1, keepdims=True) / (
        H * norm_mean * norm_mean
    )
    of_upstream = gain[...] * scaled + 1.0
    of_gelu = norm_grad / channel_norm
    gain_term = sums[1:2, :] * scaled
    shift_term = shift[...]
    copies = []
    for p, (start, stop) in enumerate(zip(CUTS[:-1], CUTS[1:])):
        for k in range(start, stop):
            cols = slice(k * LANES, (k + 1) * LANES)
            upstream = out_grad[:, cols].astype(jnp.float32)
            act_grad = upstream * of_upstream[:, cols] + gelu[:, cols] * of_gelu[:, cols]
            rounded = (act_grad * slope[:, cols]).astype(jnp.bfloat16)
            pre_grad[:, cols] = rounded
            turned[cols, :] = rounded.astype(jnp.float32).T
        cols = pl.ds(start * LANES, (stop - start) * LANES)
        copies.append(pltpu.make_async_copy(pre_grad.at[:, cols], result.at[:, cols], sems.at[p]))
        copies[-1].start()
    both = jnp.concatenate([gain_term, shift_term, jnp.zeros((6, H), jnp.float32)], axis=0)
    for b in range(H // BLOCK):
        tile, start = divmod(b * BLOCK, LANES)
        window = both[:, tile * LANES : min((tile + 2) * LANES, H)]
        if start:
            window = pltpu.roll(window, window.shape[1] - start, 1)
        gains[b : b + 1, :] = window[0:1, :LANES]
        shifts[b : b + 1, :] = window[1:2, :LANES]
    core, x = lax.axis_index("core"), lax.axis_index("x")
    y = 2 * lax.axis_index("yh") + lax.axis_index("yl")
    for of_other in range(2):
        to = core if of_other == 0 else 1 - core
        mine, beside_mine = jnp.where(to == 0, x, y), jnp.where(to == 0, y, x)
        for j in range(4):
            chunk, top = (cross if of_other else keep), j * PART
            d = lax.rem(mine + j, 4)
            for i in range(4):
                e = lax.rem(beside_mine + i, 4)
                block_x, block_y = jnp.where(to == 0, d, e), jnp.where(to == 0, e, d)
                b = (block_y // 2) * 16 + to * 8 + block_x * 2 + lax.rem(block_y, 2)
                start = pl.multiple_of(b * BLOCK, 8)
                units = turned[pl.ds(start, BLOCK), :]
                chunk[top + i * HALF : top + (i + 1) * HALF, :] = units[:HALF]
                chunk[top + FIRST + i * HALF : top + FIRST + (i + 1) * HALF, :] = units[HALF:]
                row = top + 4 * HALF + i
                chunk[row : row + 1, :] = gains[pl.ds(b, 1), :]
                chunk[row + 4 : row + 5, :] = shifts[pl.ds(b, 1), :]
    cross[4 * PART :, :] = wide[...]
    for copy in copies:
        copy.wait()


def merge(keep, arrived, *outs):
    for j in range(4):
        first, second = outs[j], outs[4 + j]
        for n, source in enumerate((keep, arrived)):
            middle = j * PART + FIRST
            first[n * FIRST : (n + 1) * FIRST, :] = source[j * PART : middle, :]
            second[n * SECOND : (n + 1) * SECOND, :] = source[middle : middle + SECOND, :]


def product(half, here, above, below, opposite, right_first, right_second, right_rest, *rest):
    if half == 0:
        outs, terms, lefts = rest[:4], rest[4], rest[5:]
    else:
        terms, outs, lefts = rest[0], rest[1:5], rest[5:]
    step = FIRST if half == 0 else SECOND
    one, two = slice(0, 4 * HALF), slice(step, step + 4 * HALF)
    sources = (
        (here[one, :], above[one, :], below[two, :]),
        (above[two, :], below[one, :]),
        (here[two, :], opposite[one, :], opposite[two, :]),
    )
    for left, values in zip(lefts, sources):
        for s, value in enumerate(values):
            left[:, s * ROWS : (s + 1) * ROWS] = value.astype(jnp.bfloat16)
    rights = (right_first, right_second, right_rest)
    across_pixels = (((1,), (1,)), ((), ()))
    if half == 0:
        small = jnp.zeros((8, LANES), jnp.float32)
        for pair in (here, above, below, opposite):
            small = small + (pair[4 * HALF : FIRST, :] + pair[FIRST + 4 * HALF :, :])
        terms[...] = small
    else:
        small = terms[...]
    bias = 0.0
    for left in lefts:
        ones = jnp.ones((8, left.shape[1]), jnp.bfloat16)
        bias = bias + lax.dot_general(ones, left[...], across_pixels, preferred_element_type=jnp.float32)
    bias = jnp.concatenate([bias, jnp.zeros((8, 3 * LANES - 4 * HALF), jnp.float32)], axis=1)
    rows = []
    for i in range(4):
        tile, start = divmod(i * HALF, LANES)
        window = bias[:, tile * LANES : (tile + 2) * LANES]
        rows.append((pltpu.roll(window, 2 * LANES - start, 1) if start else window)[0:1, :LANES])
    bias = jnp.concatenate([*rows, *rows], axis=0)
    for z in range(4):
        skip = (4 * half + z) * OWN
        turned = pltpu.roll(small, LANES - skip, 1) if skip else small
        turned_bias = pltpu.roll(bias, LANES - z * OWN, 1) if z else bias
        for i, out in enumerate(outs):
            row = z * PACKED + 61
            out[row : row + 1, :] = turned_bias[i : i + 1, :]
            out[row + 1 : row + 2, :] = turned[i : i + 1, :]
            out[row + 2 : row + 3, :] = turned[4 + i : 5 + i, :]
    for group in range(3):
        cols = slice(2 * group * LANES, min(2 * (group + 1) * LANES, C))
        total = 0.0
        for left, right in zip(lefts, rights):
            total = total + lax.dot_general(
                left[...], right[cols, :], across_pixels, preferred_element_type=jnp.float32
            )
        if group == 2:
            last = total[:, LANES:]
            last = jnp.concatenate([last, last], axis=1)
            last = jnp.concatenate([last, jnp.zeros((8, LANES), jnp.float32)], axis=0)
            left_half = lax.broadcasted_iota(jnp.int32, (6, LANES), 1) < 64
        for i, out in enumerate(outs):
            for z in range(4):
                unit = i * HALF + z * OWN
                for k in range(2 * group, min(2 * group + 2, 5)):
                    row, col = z * PACKED + k * OWN, (k - 2 * group) * LANES
                    out[row : row + OWN, :] = total[unit : unit + OWN, col : col + LANES]
                if group == 2:
                    row = z * PACKED + 5 * OWN
                    out[row : row + 6, :] = jnp.where(left_half, last[unit : unit + 6], last[unit + 6 : unit + 12])


PACKED = 64


def add(a, b, c, d, out):
    out[...] = (a[...] + b[...]) + (c[...] + d[...])


def add_below(above, a, b, c, d, out):
    out[:4] = above[...].reshape(4, PACKED, LANES)
    out[4:] = ((a[...] + b[...]) + (c[...] + d[...])).reshape(4, PACKED, LANES)


def finish(parts, weight, gain, shift, bias):
    total = parts[0]
    for z in range(1, 8):
        total = total + parts[z]
    for k in range(5):
        weight[:, k * LANES : (k + 1) * LANES] = total[k * OWN : (k + 1) * OWN, :]
    last = total[5 * OWN : 5 * OWN + 6, :]
    weight[:6, 5 * LANES :] = last[:, :64]
    weight[6:, 5 * LANES :] = last[:5, 64:]
    bias[...] = total[61:62, :OWN]
    gain[...] = total[62:63, :OWN]
    shift[...] = total[63:64, :OWN]


def on_device(normed, pre_gelu, out_grad, grn_gain):
    bf16 = jnp.bfloat16
    normed, pre_gelu, out_grad = (
        pltpu.with_memory_space_constraint(v, pltpu.HBM) for v in (normed.T, pre_gelu, out_grad)
    )
    wide = call(
        widen,
        f32(C, ROWS),
        scratch=[pltpu.VMEM((C, ROWS), bf16), pltpu.SemaphoreType.DMA((2,))],
        moved=540_000,
        in_specs=[pl.BlockSpec(memory_space=pl.ANY)],
    )(normed)
    sums, shift, gelu, slope, upstream = call(
        statistics,
        [f32(2, H), f32(1, H), f32(ROWS, H), f32(ROWS, H), jax.ShapeDtypeStruct((ROWS, H), bf16)],
        scratch=[pltpu.VMEM((ROWS, H), bf16), pltpu.SemaphoreType.DMA((2, 4))],
        flops=0,
        moved=4_400_000,
        in_specs=[pl.BlockSpec(memory_space=pl.ANY)] * 2,
    )(pre_gelu, out_grad)
    other = send(sums, other_half)

    from_below = send(wide, along(1))
    from_above = send(wide, along(-1))
    below_across = send(wide, across(1))
    above_across = send(wide, across(-1))

    def right_of(*wides, flops=GUIDE):
        shape = jax.ShapeDtypeStruct((C, len(wides) * ROWS), bf16)
        return call(narrow, shape, flops=flops, moved=4_400_000)(*wides)

    pre_grad, keep, cross = call(
        gradient,
        [jax.ShapeDtypeStruct((ROWS, H), bf16), f32(4 * PART, LANES), f32(4 * PART + C, LANES)],
        out_specs=[pl.BlockSpec(memory_space=pl.ANY)] + [pl.BlockSpec(memory_space=pltpu.VMEM)] * 2,
        scratch=[
            pltpu.VMEM((ROWS, H), bf16),
            pltpu.VMEM((H, LANES), jnp.float32),
            pltpu.VMEM((H // BLOCK, LANES), jnp.float32),
            pltpu.VMEM((H // BLOCK, LANES), jnp.float32),
            pltpu.SemaphoreType.DMA((4,)),
        ],
        flops=0,
        moved=6_000_000,
    )(sums, other, shift, grn_gain.reshape(1, H), upstream, gelu, slope, wide)
    arrived = send(cross, other_core)
    right_first = right_of(wide, from_below, above_across, flops=GUIDE)
    arrived, right_first = lax.optimization_barrier((arrived, right_first))
    firsts_and_seconds = call(
        merge, [f32(2 * FIRST, LANES)] * 4 + [f32(2 * SECOND, LANES)] * 4, moved=4_400_000
    )(keep, arrived)
    far = send(from_below, along(1))
    far_across = send(above_across, along(-1))
    firsts, seconds = list(firsts_and_seconds[:4]), list(firsts_and_seconds[4:])
    firsts[1], from_above, below_across = lax.optimization_barrier((firsts[1], from_above, below_across))
    right_second = right_of(below_across, from_above, flops=GUIDE)
    right_rest = right_of(arrived, far, far_across, flops=GUIDE)

    def around(own, one, two, three):
        return own, send(one, along(1)), send(three, along(-1)), send(two, along(2))

    def multiply(half, parts, terms=(), flops=0):
        outs = [f32(4 * PACKED, LANES)] * 4 + ([f32(8, LANES)] if half == 0 else [])
        return call(
            functools.partial(product, half),
            outs,
            scratch=[pltpu.VMEM((4 * HALF, n * ROWS), bf16) for n in (3, 2, 3)],
            flops=flops,
            moved=4_000_000,
        )(*parts, right_first, right_second, right_rest, *terms)

    def reduce_beside(own, one, two, three):
        return own, send(two, beside(2)), send(one, beside(1)), send(three, beside(-1))

    *products, terms = multiply(0, around(*firsts), flops=GUIDE)
    rows = reduce_beside(*products)
    rows = call(add, f32(4 * PACKED, LANES), flops=GUIDE//10, moved=700_000)(*rows)
    others = reduce_beside(*multiply(1, around(*seconds), (terms,), flops=GUIDE))
    rows = call(add_below, f32(8, PACKED, LANES), moved=1_000_000)(rows, *others)
    rows = lax.all_to_all(rows, "z", 0, 0, tiled=True)
    weight, gain, shift, bias = call(
        finish, [f32(OWN, C), f32(1, OWN), f32(1, OWN), f32(1, OWN)], moved=330_000
    )(rows)
    return pre_grad, weight, gain.reshape(OWN), shift.reshape(OWN), bias.reshape(OWN)


def solution(mesh):
    split = Mesh(mesh.devices.reshape(SIZES), AXES)
    return jax.shard_map(
        on_device,
        mesh=split,
        in_specs=(P(AXES, None), P(AXES, None), P(AXES, None), P()),
        out_specs=(P(AXES, None), P(AXES, None), P(AXES), P(AXES), P(AXES)),
        check_vma=False,
    )
```

```python
import functools

import jax
import jax.numpy as jnp
import numpy as np
from jax import lax
from jax.experimental import pallas as pl
from jax.experimental.pallas import tpu as pltpu
from jax.sharding import Mesh, PartitionSpec as P

root_half = 0.7071067811865476
inv_root_two_pi = 0.3989422804014327

AXES = ("yh", "core", "x", "yl", "z")
SIZES = (2, 2, 4, 2, 8)
ROWS = 128
C = 704
H = 2816
BLOCK = 88
OWN = 11
DEVICES = (4, 8 - 4)
UNITS = tuple(n * OWN for n in DEVICES)
FIRST = 4 * UNITS[0] + 8
SECOND = 4 * UNITS[1]
PART = FIRST + SECOND
LANES = 128
MIB = 1 << 20
GUIDE = 20_000_000_000


def pairs(target):
    found = []
    for i in range(256):
        yh, core, x, yl, z = (int(v) for v in np.unravel_index(i, SIZES))
        core2, x2, y2, z2 = target(core, x, 2 * yh + yl, z)
        place = (y2 // 2 % 2, core2 % 2, x2 % 4, y2 % 2, z2 % 8)
        found.append((i, int(np.ravel_multi_index(place, SIZES))))
    return found


def send(value, target):
    return lax.ppermute(value, AXES, pairs(target))


def other_core(core, x, y, z):
    return 1 - core, x, y, z


def other_half(core, x, y, z):
    return core, x, y, z ^ 1


def along(k):
    return lambda core, x, y, z: (core, x + k, y, z) if core == 0 else (core, x, y + k, z)


def across(k):
    return lambda core, x, y, z: (1, x, y + k, z) if core == 0 else (0, x + k, y, z)


def beside(k):
    return lambda core, x, y, z: (core, x, y + k, z) if core == 0 else (core, x + k, y, z)


def call(body, out_shape, scratch=(), flops=0, moved=0, limit=24, **specs):
    return pl.pallas_call(
        body,
        out_shape=out_shape,
        **specs,
        scratch_shapes=scratch,
        compiler_params=pltpu.CompilerParams(vmem_limit_bytes=limit * MIB),
        cost_estimate=pl.CostEstimate(flops=flops, bytes_accessed=moved, transcendentals=0),
    )


def f32(*shape):
    return jax.ShapeDtypeStruct(shape, jnp.float32)


def narrow(*refs):
    *wides, out = refs
    for s, wide in enumerate(wides):
        top = wide.shape[0] - C
        out[:, s * ROWS : (s + 1) * ROWS] = wide[top:, :].astype(jnp.bfloat16)


CUTS = (0, 6, 12, 17, 22)


def widen(normed_hbm, wide, normed, sems):
    half = C // 2
    copies = [
        pltpu.make_async_copy(normed_hbm.at[pl.ds(p * half, half)], normed.at[pl.ds(p * half, half)], sems.at[p])
        for p in range(2)
    ]
    for copy in copies:
        copy.start()
    for p, copy in enumerate(copies):
        copy.wait()
        rows = slice(p * half, (p + 1) * half)
        wide[rows, :] = normed[rows, :].astype(jnp.float32)


def statistics(pre_gelu_hbm, out_grad_hbm, sums, shift, gelu, slope, out_grad, pre_gelu, sems):
    copies = []
    for p, (start, stop) in enumerate(zip(CUTS[:-1], CUTS[1:])):
        cols = pl.ds(start * LANES, (stop - start) * LANES)
        for n, (source, target) in enumerate(((pre_gelu_hbm, pre_gelu), (out_grad_hbm, out_grad))):
            copies.append(pltpu.make_async_copy(source.at[:, cols], target.at[:, cols], sems.at[n, p]))
            copies[-1].start()
    for p, (start, stop) in enumerate(zip(CUTS[:-1], CUTS[1:])):
        copies[2 * p].wait()
        copies[2 * p + 1].wait()
        for k in range(start, stop):
            cols = slice(k * LANES, (k + 1) * LANES)
            values = pre_gelu[:, cols].astype(jnp.float32)
            upstream = out_grad[:, cols].astype(jnp.float32)
            cdf = 0.5 * (1.0 + lax.erf(values * root_half))
            gelu_out = values * cdf
            gelu[:, cols] = gelu_out
            slope[:, cols] = cdf + values * jnp.exp(-0.5 * values * values) * inv_root_two_pi
            sums[0:1, cols] = jnp.sum(gelu_out * gelu_out, axis=0, keepdims=True)
            sums[1:2, cols] = jnp.sum(upstream * gelu_out, axis=0, keepdims=True)
            shift[0:1, cols] = jnp.sum(upstream, axis=0, keepdims=True)


def gradient(sums, other, shift, gain, out_grad, gelu, slope, wide, pre_grad, keep, cross, *scratch):
    turned, gains, shifts = scratch
    squares = sums[0:1, :] + other[0:1, :]
    response = sums[1:2, :] + other[1:2, :]
    channel_norm = jnp.sqrt(squares + 1e-06)
    norm_mean = jnp.sum(channel_norm, axis=1, keepdims=True) * (1.0 / H) + 1e-06
    scaled = channel_norm / norm_mean
    scaled_grad = gain[...] * response
    norm_grad = scaled_grad / norm_mean - jnp.sum(scaled_grad * channel_norm, axis=1, keepdims=True) / (
        H * norm_mean * norm_mean
    )
    of_upstream = gain[...] * scaled + 1.0
    of_gelu = norm_grad / channel_norm
    gain_term = sums[1:2, :] * scaled
    shift_term = shift[...]
    for k in range(H // LANES):
        cols = slice(k * LANES, (k + 1) * LANES)
        upstream = out_grad[:, cols].astype(jnp.float32)
        act_grad = upstream * of_upstream[:, cols] + gelu[:, cols] * of_gelu[:, cols]
        rounded = (act_grad * slope[:, cols]).astype(jnp.bfloat16)
        pre_grad[:, cols] = rounded
        turned[cols, :] = rounded.astype(jnp.float32).T
    both = jnp.concatenate([gain_term, shift_term, jnp.zeros((6, H), jnp.float32)], axis=0)
    for b in range(H // BLOCK):
        tile, start = divmod(b * BLOCK, LANES)
        window = both[:, tile * LANES : min((tile + 2) * LANES, H)]
        if start:
            window = pltpu.roll(window, window.shape[1] - start, 1)
        gains[b : b + 1, :] = window[0:1, :LANES]
        shifts[b : b + 1, :] = window[1:2, :LANES]
    core, x = lax.axis_index("core"), lax.axis_index("x")
    y = 2 * lax.axis_index("yh") + lax.axis_index("yl")
    for of_other in range(2):
        to = core if of_other == 0 else 1 - core
        mine, beside_mine = jnp.where(to == 0, x, y), jnp.where(to == 0, y, x)
        for j in range(4):
            chunk, top = (cross if of_other else keep), j * PART
            d = lax.rem(mine + j, 4)
            for i in range(4):
                e = lax.rem(beside_mine + i, 4)
                block_x, block_y = jnp.where(to == 0, d, e), jnp.where(to == 0, e, d)
                b = (block_y // 2) * 16 + to * 8 + block_x * 2 + lax.rem(block_y, 2)
                start = pl.multiple_of(b * BLOCK, 8)
                units = turned[pl.ds(start, BLOCK), :]
                row = top + i * UNITS[0]
                chunk[row : row + UNITS[0], :] = units[: UNITS[0]]
                row = top + FIRST + i * UNITS[1]
                chunk[row : row + UNITS[1], :] = units[UNITS[0] :]
                row = top + 4 * UNITS[0] + i
                chunk[row : row + 1, :] = gains[pl.ds(b, 1), :]
                chunk[row + 4 : row + 5, :] = shifts[pl.ds(b, 1), :]
    cross[4 * PART :, :] = wide[...]


def store(value, result, sems):
    parts = sems.shape[0]
    rows = ROWS // parts
    copies = [
        pltpu.make_async_copy(value.at[pl.ds(p * rows, rows)], result.at[pl.ds(p * rows, rows)], sems.at[p])
        for p in range(parts)
    ]
    for copy in copies:
        copy.start()
    for copy in copies:
        copy.wait()


def merge(keep, arrived, *outs):
    for j in range(4):
        first, second = outs[j], outs[4 + j]
        for n, source in enumerate((keep, arrived)):
            middle = j * PART + FIRST
            first[n * FIRST : (n + 1) * FIRST, :] = source[j * PART : middle, :]
            second[n * SECOND : (n + 1) * SECOND, :] = source[middle : middle + SECOND, :]


def product(half, steps, here, *refs):
    arrived = dict(zip(steps, refs[:3]))
    above, below, opposite = arrived[1], arrived[-1], arrived[2]
    (right_first, right_second, right_rest), rest = refs[3:6], refs[6:]
    if half == 0:
        outs, terms, lefts = rest[:4], rest[4], rest[5:]
    else:
        terms, outs, lefts = rest[0], rest[1:5], rest[5:]
    step = FIRST if half == 0 else SECOND
    units = UNITS[half]
    one, two = slice(0, 4 * units), slice(step, step + 4 * units)
    sources = (
        (here[one, :], above[one, :], below[two, :]),
        (above[two, :], below[one, :]),
        (here[two, :], opposite[one, :], opposite[two, :]),
    )
    for left, values in zip(lefts, sources):
        for s, value in enumerate(values):
            below_it = jnp.zeros((left.shape[0] - 4 * units, ROWS), jnp.float32)
            value = jnp.concatenate([value, below_it], axis=0) if below_it.size else value
            left[:, s * ROWS : (s + 1) * ROWS] = value.astype(jnp.bfloat16)
    rights = (right_first, right_second, right_rest)
    across_pixels = (((1,), (1,)), ((), ()))
    if half == 0:
        small = jnp.zeros((8, LANES), jnp.float32)
        for pair in (here, above, below, opposite):
            small = small + (pair[4 * units : FIRST, :] + pair[FIRST + 4 * units :, :])
        terms[...] = small
    else:
        small = terms[...]
    bias = 0.0
    for left in lefts:
        ones = jnp.ones((8, left.shape[1]), jnp.bfloat16)
        bias = bias + lax.dot_general(ones, left[...], across_pixels, preferred_element_type=jnp.float32)
    width = (4 * units // LANES + 2) * LANES
    bias = jnp.concatenate([bias, jnp.zeros((8, width - bias.shape[1]), jnp.float32)], axis=1)
    rows = []
    for i in range(4):
        tile, start = divmod(i * units, LANES)
        window = bias[:, tile * LANES : (tile + 2) * LANES]
        rows.append((pltpu.roll(window, 2 * LANES - start, 1) if start else window)[0:1, :LANES])
    bias = jnp.concatenate([*rows, *rows], axis=0)
    for z in range(DEVICES[half]):
        skip = (DEVICES[0] * half + z) * OWN
        turned = pltpu.roll(small, LANES - skip, 1) if skip else small
        turned_bias = pltpu.roll(bias, LANES - z * OWN, 1) if z else bias
        for i, out in enumerate(outs):
            row = z * PACKED + 61
            out[row : row + 1, :] = turned_bias[i : i + 1, :]
            out[row + 1 : row + 2, :] = turned[i : i + 1, :]
            out[row + 2 : row + 3, :] = turned[4 + i : 5 + i, :]
    for group in range(3):
        cols = slice(2 * group * LANES, min(2 * (group + 1) * LANES, C))
        total = 0.0
        for left, right in zip(lefts, rights):
            total = total + lax.dot_general(
                left[...], right[cols, :], across_pixels, preferred_element_type=jnp.float32
            )
        if group == 2:
            last = total[:, LANES:]
            last = jnp.concatenate([last, last], axis=1)
            last = jnp.concatenate([last, jnp.zeros((8, LANES), jnp.float32)], axis=0)
            left_half = lax.broadcasted_iota(jnp.int32, (6, LANES), 1) < 64
        for i, out in enumerate(outs):
            for z in range(DEVICES[half]):
                unit = i * units + z * OWN
                for k in range(2 * group, min(2 * group + 2, 5)):
                    row, col = z * PACKED + k * OWN, (k - 2 * group) * LANES
                    out[row : row + OWN, :] = total[unit : unit + OWN, col : col + LANES]
                if group == 2:
                    row = z * PACKED + 5 * OWN
                    out[row : row + 6, :] = jnp.where(left_half, last[unit : unit + 6], last[unit + 6 : unit + 12])


PACKED = 64


def add(a, b, c, d, out):
    out[...] = (a[...] + b[...]) + (c[...] + d[...])


def add_below(above, a, b, c, d, out):
    out[: DEVICES[0]] = above[...].reshape(DEVICES[0], PACKED, LANES)
    out[DEVICES[0] :] = ((a[...] + b[...]) + (c[...] + d[...])).reshape(DEVICES[1], PACKED, LANES)


def finish(parts, weight, gain, shift, bias):
    total = parts[0]
    for z in range(1, 8):
        total = total + parts[z]
    for k in range(5):
        weight[:, k * LANES : (k + 1) * LANES] = total[k * OWN : (k + 1) * OWN, :]
    last = total[5 * OWN : 5 * OWN + 6, :]
    weight[:6, 5 * LANES :] = last[:, :64]
    weight[6:, 5 * LANES :] = last[:5, 64:]
    bias[...] = total[61:62, :OWN]
    gain[...] = total[62:63, :OWN]
    shift[...] = total[63:64, :OWN]


def on_device(normed, pre_gelu, out_grad, grn_gain):
    bf16 = jnp.bfloat16
    normed, pre_gelu, out_grad = (
        pltpu.with_memory_space_constraint(v, pltpu.HBM) for v in (normed.T, pre_gelu, out_grad)
    )
    wide = call(
        widen,
        f32(C, ROWS),
        scratch=[pltpu.VMEM((C, ROWS), bf16), pltpu.SemaphoreType.DMA((2,))],
        moved=540_000,
        in_specs=[pl.BlockSpec(memory_space=pl.ANY)],
    )(normed)
    sums, shift, gelu, slope, upstream = call(
        statistics,
        [f32(2, H), f32(1, H), f32(ROWS, H), f32(ROWS, H), jax.ShapeDtypeStruct((ROWS, H), bf16)],
        scratch=[pltpu.VMEM((ROWS, H), bf16), pltpu.SemaphoreType.DMA((2, 4))],
        flops=0,
        moved=4_400_000,
        in_specs=[pl.BlockSpec(memory_space=pl.ANY)] * 2,
    )(pre_gelu, out_grad)
    other = send(sums, other_half)

    from_below = send(wide, along(1))
    from_above = send(wide, along(-1))
    below_across = send(wide, across(1))
    above_across = send(wide, across(-1))

    def right_of(*wides, flops=GUIDE):
        shape = jax.ShapeDtypeStruct((C, len(wides) * ROWS), bf16)
        return call(narrow, shape, flops=flops, moved=4_400_000)(*wides)

    pre_grad, keep, cross = call(
        gradient,
        [jax.ShapeDtypeStruct((ROWS, H), bf16), f32(4 * PART, LANES), f32(4 * PART + C, LANES)],
        scratch=[
            pltpu.VMEM((H, LANES), jnp.float32),
            pltpu.VMEM((H // BLOCK, LANES), jnp.float32),
            pltpu.VMEM((H // BLOCK, LANES), jnp.float32),
        ],
        flops=0,
        moved=6_000_000,
    )(sums, other, shift, grn_gain.reshape(1, H), upstream, gelu, slope, wide)
    arrived = send(cross, other_core)
    right_first = right_of(wide, from_below, above_across, flops=GUIDE)
    arrived, right_first = lax.optimization_barrier((arrived, right_first))
    firsts_and_seconds = call(
        merge, [f32(2 * FIRST, LANES)] * 4 + [f32(2 * SECOND, LANES)] * 4, moved=4_400_000
    )(keep, arrived)
    far = send(from_below, along(1))
    far_across = send(above_across, along(-1))
    firsts, seconds = list(firsts_and_seconds[:4]), list(firsts_and_seconds[4:])
    firsts[1], below_across, from_above = lax.optimization_barrier((firsts[1], below_across, from_above))
    right_second = right_of(below_across, from_above, flops=GUIDE)
    right_rest = right_of(arrived, far, far_across, flops=GUIDE)

    def around(steps, own, *away):
        return own, *(send(away[(step - 1) % 4], along(step)) for step in steps)

    def multiply(half, steps, parts, terms=(), flops=0):
        outs = [f32(DEVICES[half] * PACKED, LANES)] * 4 + ([f32(8, LANES)] if half == 0 else [])
        return call(
            functools.partial(product, half, steps),
            outs,
            scratch=[pltpu.VMEM(((4 * UNITS[half] + 15) // 16 * 16, n * ROWS), bf16) for n in (3, 2, 3)],
            flops=flops,
            moved=4_000_000,
        )(*around(steps, *parts), right_first, right_second, right_rest, *terms)

    def reduce_beside(steps, own, *away):
        return own, *(send(away[(step - 1) % 4], beside(step)) for step in steps)

    *products, terms = multiply(0, (1, -1, 2), firsts, flops=GUIDE)
    rows = reduce_beside((2, 1, -1), *products)
    rows = call(add, f32(DEVICES[0] * PACKED, LANES), flops=GUIDE//10, moved=700_000)(*rows)
    rows, pre_grad = lax.optimization_barrier((rows, pre_grad))
    pre_grad = call(
        store,
        jax.ShapeDtypeStruct((ROWS, H), bf16),
        scratch=[pltpu.SemaphoreType.DMA((4,))],
        moved=1_440_000,
        in_specs=[pl.BlockSpec(memory_space=pltpu.VMEM)],
        out_specs=pl.BlockSpec(memory_space=pl.ANY),
    )(pre_grad)
    rows, pre_grad = lax.optimization_barrier((rows, pre_grad))
    others = reduce_beside((2, 1, -1), *multiply(1, (1, -1, 2), seconds, (terms,), flops=GUIDE))
    rows = call(add_below, f32(8, PACKED, LANES), moved=1_000_000)(rows, *others)
    rows = lax.all_to_all(rows, "z", 0, 0, tiled=True)
    weight, gain, shift, bias = call(
        finish, [f32(OWN, C), f32(1, OWN), f32(1, OWN), f32(1, OWN)], moved=330_000
    )(rows)
    return pre_grad, weight, gain.reshape(OWN), shift.reshape(OWN), bias.reshape(OWN)


def solution(mesh):
    split = Mesh(mesh.devices.reshape(SIZES), AXES)
    return jax.shard_map(
        on_device,
        mesh=split,
        in_specs=(P(AXES, None), P(AXES, None), P(AXES, None), P()),
        out_specs=(P(AXES, None), P(AXES, None), P(AXES), P(AXES), P(AXES)),
        check_vma=False,
    )
```

```python
import functools

import jax
import jax.numpy as jnp
import numpy as np
from jax import lax
from jax.experimental import pallas as pl
from jax.experimental.pallas import tpu as pltpu
from jax.sharding import Mesh, PartitionSpec as P

root_half = 0.7071067811865476
inv_root_two_pi = 0.3989422804014327

AXES = ("yh", "core", "x", "yl", "z")
SIZES = (2, 2, 4, 2, 8)
ROWS = 128
C = 704
H = 2816
BLOCK = 88
OWN = 11
STEPS = ((1, 2), (3, 0))
FIRST = len(STEPS[0]) * BLOCK + 8
SECOND = len(STEPS[1]) * BLOCK
PART = FIRST + SECOND
LANES = 128
MIB = 1 << 20
GUIDE = 20_000_000_000


def pairs(target):
    found = []
    for i in range(256):
        yh, core, x, yl, z = (int(v) for v in np.unravel_index(i, SIZES))
        core2, x2, y2, z2 = target(core, x, 2 * yh + yl, z)
        place = (y2 // 2 % 2, core2 % 2, x2 % 4, y2 % 2, z2 % 8)
        found.append((i, int(np.ravel_multi_index(place, SIZES))))
    return found


def send(value, target):
    return lax.ppermute(value, AXES, pairs(target))


def other_core(core, x, y, z):
    return 1 - core, x, y, z


def other_half(core, x, y, z):
    return core, x, y, z ^ 1


def along(k):
    return lambda core, x, y, z: (core, x + k, y, z) if core == 0 else (core, x, y + k, z)


def across(k):
    return lambda core, x, y, z: (1, x, y + k, z) if core == 0 else (0, x + k, y, z)


def beside(k):
    return lambda core, x, y, z: (core, x, y + k, z) if core == 0 else (core, x + k, y, z)


def call(body, out_shape, scratch=(), flops=0, moved=0, limit=24, **specs):
    return pl.pallas_call(
        body,
        out_shape=out_shape,
        **specs,
        scratch_shapes=scratch,
        compiler_params=pltpu.CompilerParams(vmem_limit_bytes=limit * MIB),
        cost_estimate=pl.CostEstimate(flops=flops, bytes_accessed=moved, transcendentals=0),
    )


def f32(*shape):
    return jax.ShapeDtypeStruct(shape, jnp.float32)


def narrow(*refs):
    *wides, out = refs
    for s, wide in enumerate(wides):
        top = wide.shape[0] - C
        out[:, s * ROWS : (s + 1) * ROWS] = wide[top:, :].astype(jnp.bfloat16)


CUTS = (0, 6, 12, 17, 22)


def widen(normed_hbm, wide, normed, sems):
    half = C // 2
    copies = [
        pltpu.make_async_copy(normed_hbm.at[pl.ds(p * half, half)], normed.at[pl.ds(p * half, half)], sems.at[p])
        for p in range(2)
    ]
    for copy in copies:
        copy.start()
    for p, copy in enumerate(copies):
        copy.wait()
        rows = slice(p * half, (p + 1) * half)
        wide[rows, :] = normed[rows, :].astype(jnp.float32)


def statistics(pre_gelu_hbm, out_grad_hbm, sums, shift, gelu, slope, out_grad, pre_gelu, sems):
    copies = []
    for p, (start, stop) in enumerate(zip(CUTS[:-1], CUTS[1:])):
        cols = pl.ds(start * LANES, (stop - start) * LANES)
        for n, (source, target) in enumerate(((pre_gelu_hbm, pre_gelu), (out_grad_hbm, out_grad))):
            copies.append(pltpu.make_async_copy(source.at[:, cols], target.at[:, cols], sems.at[n, p]))
            copies[-1].start()
    for p, (start, stop) in enumerate(zip(CUTS[:-1], CUTS[1:])):
        copies[2 * p].wait()
        copies[2 * p + 1].wait()
        for k in range(start, stop):
            cols = slice(k * LANES, (k + 1) * LANES)
            values = pre_gelu[:, cols].astype(jnp.float32)
            upstream = out_grad[:, cols].astype(jnp.float32)
            cdf = 0.5 * (1.0 + lax.erf(values * root_half))
            gelu_out = values * cdf
            gelu[:, cols] = gelu_out
            slope[:, cols] = cdf + values * jnp.exp(-0.5 * values * values) * inv_root_two_pi
            sums[0:1, cols] = jnp.sum(gelu_out * gelu_out, axis=0, keepdims=True)
            sums[1:2, cols] = jnp.sum(upstream * gelu_out, axis=0, keepdims=True)
            shift[0:1, cols] = jnp.sum(upstream, axis=0, keepdims=True)


def gradient(sums, other, shift, gain, out_grad, gelu, slope, wide, pre_grad, keep, cross, *scratch):
    turned, gains, shifts = scratch
    squares = sums[0:1, :] + other[0:1, :]
    response = sums[1:2, :] + other[1:2, :]
    channel_norm = jnp.sqrt(squares + 1e-06)
    norm_mean = jnp.sum(channel_norm, axis=1, keepdims=True) * (1.0 / H) + 1e-06
    scaled = channel_norm / norm_mean
    scaled_grad = gain[...] * response
    norm_grad = scaled_grad / norm_mean - jnp.sum(scaled_grad * channel_norm, axis=1, keepdims=True) / (
        H * norm_mean * norm_mean
    )
    of_upstream = gain[...] * scaled + 1.0
    of_gelu = norm_grad / channel_norm
    gain_term = sums[1:2, :] * scaled
    shift_term = shift[...]
    for k in range(H // LANES):
        cols = slice(k * LANES, (k + 1) * LANES)
        upstream = out_grad[:, cols].astype(jnp.float32)
        act_grad = upstream * of_upstream[:, cols] + gelu[:, cols] * of_gelu[:, cols]
        rounded = (act_grad * slope[:, cols]).astype(jnp.bfloat16)
        pre_grad[:, cols] = rounded
        turned[cols, :] = rounded.astype(jnp.float32).T
    both = jnp.concatenate([gain_term, shift_term, jnp.zeros((6, H), jnp.float32)], axis=0)
    for b in range(H // BLOCK):
        tile, start = divmod(b * BLOCK, LANES)
        window = both[:, tile * LANES : min((tile + 2) * LANES, H)]
        if start:
            window = pltpu.roll(window, window.shape[1] - start, 1)
        gains[b : b + 1, :] = window[0:1, :LANES]
        shifts[b : b + 1, :] = window[1:2, :LANES]
    core, x = lax.axis_index("core"), lax.axis_index("x")
    y = 2 * lax.axis_index("yh") + lax.axis_index("yl")
    for of_other in range(2):
        to = core if of_other == 0 else 1 - core
        mine, beside_mine = jnp.where(to == 0, x, y), jnp.where(to == 0, y, x)
        for j in range(4):
            chunk, top = (cross if of_other else keep), j * PART
            d = lax.rem(mine + j, 4)
            for i in range(4):
                e = lax.rem(beside_mine + i, 4)
                block_x, block_y = jnp.where(to == 0, d, e), jnp.where(to == 0, e, d)
                b = (block_y // 2) * 16 + to * 8 + block_x * 2 + lax.rem(block_y, 2)
                start = pl.multiple_of(b * BLOCK, 8)
                units = turned[pl.ds(start, BLOCK), :]
                part = 0 if i in STEPS[0] else 1
                row = top + part * FIRST + STEPS[part].index(i) * BLOCK
                chunk[row : row + BLOCK, :] = units
                row = top + FIRST - 8 + i
                chunk[row : row + 1, :] = gains[pl.ds(b, 1), :]
                chunk[row + 4 : row + 5, :] = shifts[pl.ds(b, 1), :]
    cross[4 * PART :, :] = wide[...]


def store(value, result, sems):
    parts = sems.shape[0]
    rows = ROWS // parts
    copies = [
        pltpu.make_async_copy(value.at[pl.ds(p * rows, rows)], result.at[pl.ds(p * rows, rows)], sems.at[p])
        for p in range(parts)
    ]
    for copy in copies:
        copy.start()
    for copy in copies:
        copy.wait()


def merge(keep, arrived, *outs):
    for j in range(4):
        first, second = outs[j], outs[4 + j]
        for n, source in enumerate((keep, arrived)):
            middle = j * PART + FIRST
            first[n * FIRST : (n + 1) * FIRST, :] = source[j * PART : middle, :]
            second[n * SECOND : (n + 1) * SECOND, :] = source[middle : middle + SECOND, :]


def product(half, steps, here, *refs):
    arrived = dict(zip(steps, refs[:3]))
    above, below, opposite = arrived[1], arrived[-1], arrived[2]
    (right_first, right_second, right_rest), rest = refs[3:6], refs[6:]
    blocks = STEPS[half]
    count, height = len(blocks), len(blocks) * BLOCK
    if half == 0:
        outs, terms, lefts = rest[:count], rest[count], rest[count + 1 :]
    else:
        terms, outs, lefts = rest[0], rest[1 : count + 1], rest[count + 1 :]
    step = FIRST if half == 0 else SECOND
    one, two = slice(0, height), slice(step, step + height)
    sources = (
        (here[one, :], above[one, :], below[two, :]),
        (above[two, :], below[one, :]),
        (here[two, :], opposite[one, :], opposite[two, :]),
    )
    for left, values in zip(lefts, sources):
        for s, value in enumerate(values):
            below_it = jnp.zeros((left.shape[0] - height, ROWS), jnp.float32)
            value = jnp.concatenate([value, below_it], axis=0) if below_it.size else value
            left[:, s * ROWS : (s + 1) * ROWS] = value.astype(jnp.bfloat16)
    rights = (right_first, right_second, right_rest)
    across_pixels = (((1,), (1,)), ((), ()))
    if half == 0:
        small = jnp.zeros((8, LANES), jnp.float32)
        for pair in (here, above, below, opposite):
            small = small + (pair[height:FIRST, :] + pair[FIRST + height :, :])
        terms[...] = small
    else:
        small = terms[...]
    bias = 0.0
    for left in lefts:
        ones = jnp.ones((8, left.shape[1]), jnp.bfloat16)
        bias = bias + lax.dot_general(ones, left[...], across_pixels, preferred_element_type=jnp.float32)
    width = (height // LANES + 2) * LANES
    bias = jnp.concatenate([bias, jnp.zeros((8, width - bias.shape[1]), jnp.float32)], axis=1)
    rows = []
    for n in range(count):
        tile, start = divmod(n * BLOCK, LANES)
        window = bias[:, tile * LANES : (tile + 2) * LANES]
        rows.append((pltpu.roll(window, 2 * LANES - start, 1) if start else window)[0:1, :LANES])
    small = jnp.concatenate([small, *rows, *[rows[0]] * (8 - count)], axis=0)
    for z in range(8):
        turned = pltpu.roll(small, LANES - z * OWN, 1) if z else small
        for n, (i, out) in enumerate(zip(blocks, outs)):
            row = z * PACKED + 61
            out[row : row + 1, :] = turned[8 + n : 9 + n, :]
            out[row + 1 : row + 2, :] = turned[i : i + 1, :]
            out[row + 2 : row + 3, :] = turned[4 + i : 5 + i, :]
    for group in range(3):
        cols = slice(2 * group * LANES, min(2 * (group + 1) * LANES, C))
        total = 0.0
        for left, right in zip(lefts, rights):
            total = total + lax.dot_general(
                left[...], right[cols, :], across_pixels, preferred_element_type=jnp.float32
            )
        if group == 2:
            last = total[:, LANES:]
            last = jnp.concatenate([last, last], axis=1)
            last = jnp.concatenate([last, jnp.zeros((8, LANES), jnp.float32)], axis=0)
            left_half = lax.broadcasted_iota(jnp.int32, (6, LANES), 1) < 64
        for n, out in enumerate(outs):
            for z in range(8):
                unit = n * BLOCK + z * OWN
                for k in range(2 * group, min(2 * group + 2, 5)):
                    row, col = z * PACKED + k * OWN, (k - 2 * group) * LANES
                    out[row : row + OWN, :] = total[unit : unit + OWN, col : col + LANES]
                if group == 2:
                    row = z * PACKED + 5 * OWN
                    out[row : row + 6, :] = jnp.where(left_half, last[unit : unit + 6], last[unit + 6 : unit + 12])


PACKED = 64


def add(*refs):
    *parts, out = refs
    total = parts[0][...]
    for part in parts[1:]:
        total = total + part[...]
    out[...] = total


def finish(parts, weight, gain, shift, bias):
    total = parts[0]
    for z in range(1, 8):
        total = total + parts[z]
    for k in range(5):
        weight[:, k * LANES : (k + 1) * LANES] = total[k * OWN : (k + 1) * OWN, :]
    last = total[5 * OWN : 5 * OWN + 6, :]
    weight[:6, 5 * LANES :] = last[:, :64]
    weight[6:, 5 * LANES :] = last[:5, 64:]
    bias[...] = total[61:62, :OWN]
    gain[...] = total[62:63, :OWN]
    shift[...] = total[63:64, :OWN]


def on_device(normed, pre_gelu, out_grad, grn_gain):
    bf16 = jnp.bfloat16
    normed, pre_gelu, out_grad = (
        pltpu.with_memory_space_constraint(v, pltpu.HBM) for v in (normed.T, pre_gelu, out_grad)
    )
    wide = call(
        widen,
        f32(C, ROWS),
        scratch=[pltpu.VMEM((C, ROWS), bf16), pltpu.SemaphoreType.DMA((2,))],
        moved=540_000,
        in_specs=[pl.BlockSpec(memory_space=pl.ANY)],
    )(normed)
    sums, shift, gelu, slope, upstream = call(
        statistics,
        [f32(2, H), f32(1, H), f32(ROWS, H), f32(ROWS, H), jax.ShapeDtypeStruct((ROWS, H), bf16)],
        scratch=[pltpu.VMEM((ROWS, H), bf16), pltpu.SemaphoreType.DMA((2, 4))],
        flops=0,
        moved=4_400_000,
        in_specs=[pl.BlockSpec(memory_space=pl.ANY)] * 2,
    )(pre_gelu, out_grad)
    other = send(sums, other_half)

    from_below = send(wide, along(1))
    from_above = send(wide, along(-1))
    below_across = send(wide, across(1))
    above_across = send(wide, across(-1))

    def right_of(*wides, flops=GUIDE):
        shape = jax.ShapeDtypeStruct((C, len(wides) * ROWS), bf16)
        return call(narrow, shape, flops=flops, moved=4_400_000)(*wides)

    pre_grad, keep, cross = call(
        gradient,
        [jax.ShapeDtypeStruct((ROWS, H), bf16), f32(4 * PART, LANES), f32(4 * PART + C, LANES)],
        scratch=[
            pltpu.VMEM((H, LANES), jnp.float32),
            pltpu.VMEM((H // BLOCK, LANES), jnp.float32),
            pltpu.VMEM((H // BLOCK, LANES), jnp.float32),
        ],
        flops=0,
        moved=6_000_000,
    )(sums, other, shift, grn_gain.reshape(1, H), upstream, gelu, slope, wide)
    arrived = send(cross, other_core)
    right_first = right_of(wide, from_below, above_across, flops=GUIDE)
    arrived, right_first = lax.optimization_barrier((arrived, right_first))
    firsts_and_seconds = call(
        merge, [f32(2 * FIRST, LANES)] * 4 + [f32(2 * SECOND, LANES)] * 4, moved=4_400_000
    )(keep, arrived)
    far = send(from_below, along(1))
    far_across = send(above_across, along(-1))
    firsts, seconds = list(firsts_and_seconds[:4]), list(firsts_and_seconds[4:])
    firsts[1], below_across, from_above = lax.optimization_barrier((firsts[1], below_across, from_above))
    right_second = right_of(below_across, from_above, flops=GUIDE)
    right_rest = right_of(arrived, far, far_across, flops=GUIDE)

    def around(steps, own, *away):
        return own, *(send(away[(step - 1) % 4], along(step)) for step in steps)

    def multiply(half, steps, parts, terms=(), flops=0):
        count = len(STEPS[half])
        outs = [f32(8 * PACKED, LANES)] * count + ([f32(8, LANES)] if half == 0 else [])
        height = (count * BLOCK + 15) // 16 * 16
        return call(
            functools.partial(product, half, steps),
            outs,
            scratch=[pltpu.VMEM((height, n * ROWS), bf16) for n in (3, 2, 3)],
            flops=flops,
            moved=4_000_000,
        )(*around(steps, *parts), right_first, right_second, right_rest, *terms)

    def reduce_beside(half, products):
        return [value if i == 0 else send(value, beside(-1 if i == 3 else i)) for i, value in zip(STEPS[half], products)]

    def add_up(*values, flops=0):
        return call(add, f32(8 * PACKED, LANES), flops=flops, moved=700_000)(*values)

    *products, terms = multiply(0, (1, -1, 2), firsts, flops=GUIDE)
    rows = add_up(*reduce_beside(0, products), flops=GUIDE // 10)
    rows, pre_grad = lax.optimization_barrier((rows, pre_grad))
    pre_grad = call(
        store,
        jax.ShapeDtypeStruct((ROWS, H), bf16),
        scratch=[pltpu.SemaphoreType.DMA((4,))],
        moved=1_440_000,
        in_specs=[pl.BlockSpec(memory_space=pltpu.VMEM)],
        out_specs=pl.BlockSpec(memory_space=pl.ANY),
    )(pre_grad)
    rows, pre_grad = lax.optimization_barrier((rows, pre_grad))
    others = multiply(1, (1, -1, 2), seconds, (terms,), flops=GUIDE)
    rows = add_up(rows, *reduce_beside(1, others))
    rows = lax.all_to_all(rows.reshape(8, PACKED, LANES), "z", 0, 0, tiled=True)
    weight, gain, shift, bias = call(
        finish, [f32(OWN, C), f32(1, OWN), f32(1, OWN), f32(1, OWN)], moved=330_000
    )(rows)
    return pre_grad, weight, gain.reshape(OWN), shift.reshape(OWN), bias.reshape(OWN)


def solution(mesh):
    split = Mesh(mesh.devices.reshape(SIZES), AXES)
    return jax.shard_map(
        on_device,
        mesh=split,
        in_specs=(P(AXES, None), P(AXES, None), P(AXES, None), P()),
        out_specs=(P(AXES, None), P(AXES, None), P(AXES), P(AXES), P(AXES)),
        check_vma=False,
    )
```

```python
import functools

import jax
import jax.numpy as jnp
import numpy as np
from jax import lax
from jax.experimental import pallas as pl
from jax.experimental.pallas import tpu as pltpu
from jax.sharding import Mesh, PartitionSpec as P

root_half = 0.7071067811865476
inv_root_two_pi = 0.3989422804014327

AXES = ("yh", "core", "x", "yl", "z")
SIZES = (2, 2, 4, 2, 8)
ROWS = 128
C = 704
H = 2816
BLOCK = 88
OWN = 11
STEPS = ((1, 2), (3, 0))
FIRST = len(STEPS[0]) * BLOCK + 8
SECOND = len(STEPS[1]) * BLOCK
PART = FIRST + SECOND
LANES = 128
MIB = 1 << 20
GUIDE = 20_000_000_000


def pairs(target):
    found = []
    for i in range(256):
        yh, core, x, yl, z = (int(v) for v in np.unravel_index(i, SIZES))
        core2, x2, y2, z2 = target(core, x, 2 * yh + yl, z)
        place = (y2 // 2 % 2, core2 % 2, x2 % 4, y2 % 2, z2 % 8)
        found.append((i, int(np.ravel_multi_index(place, SIZES))))
    return found


def send(value, target):
    return lax.ppermute(value, AXES, pairs(target))


def other_core(core, x, y, z):
    return 1 - core, x, y, z


def other_half(core, x, y, z):
    return core, x, y, z ^ 1


def along(k):
    return lambda core, x, y, z: (core, x + k, y, z) if core == 0 else (core, x, y + k, z)


def across(k):
    return lambda core, x, y, z: (1, x, y + k, z) if core == 0 else (0, x + k, y, z)


def beside(k):
    return lambda core, x, y, z: (core, x, y + k, z) if core == 0 else (core, x + k, y, z)


def call(body, out_shape, scratch=(), flops=0, moved=0, limit=24, **specs):
    return pl.pallas_call(
        body,
        out_shape=out_shape,
        **specs,
        scratch_shapes=scratch,
        compiler_params=pltpu.CompilerParams(vmem_limit_bytes=limit * MIB),
        cost_estimate=pl.CostEstimate(flops=flops, bytes_accessed=moved, transcendentals=0),
    )


def f32(*shape):
    return jax.ShapeDtypeStruct(shape, jnp.float32)


def narrow(*refs):
    *wides, out = refs
    for s, wide in enumerate(wides):
        top = wide.shape[0] - C
        out[s * ROWS : (s + 1) * ROWS, :] = wide[top:, :].T.astype(jnp.bfloat16)


CUTS = (0, 6, 12, 17, 22)


def widen(normed_hbm, wide, normed, sems):
    half = C // 2
    copies = [
        pltpu.make_async_copy(normed_hbm.at[pl.ds(p * half, half)], normed.at[pl.ds(p * half, half)], sems.at[p])
        for p in range(2)
    ]
    for copy in copies:
        copy.start()
    for p, copy in enumerate(copies):
        copy.wait()
        rows = slice(p * half, (p + 1) * half)
        wide[rows, :] = normed[rows, :].astype(jnp.float32)


def statistics(pre_gelu_hbm, out_grad_hbm, sums, shift, gelu, slope, out_grad, pre_gelu, sems):
    copies = []
    for p, (start, stop) in enumerate(zip(CUTS[:-1], CUTS[1:])):
        cols = pl.ds(start * LANES, (stop - start) * LANES)
        for n, (source, target) in enumerate(((pre_gelu_hbm, pre_gelu), (out_grad_hbm, out_grad))):
            copies.append(pltpu.make_async_copy(source.at[:, cols], target.at[:, cols], sems.at[n, p]))
            copies[-1].start()
    for p, (start, stop) in enumerate(zip(CUTS[:-1], CUTS[1:])):
        copies[2 * p].wait()
        copies[2 * p + 1].wait()
        for k in range(start, stop):
            cols = slice(k * LANES, (k + 1) * LANES)
            values = pre_gelu[:, cols].astype(jnp.float32)
            upstream = out_grad[:, cols].astype(jnp.float32)
            cdf = 0.5 * (1.0 + lax.erf(values * root_half))
            gelu_out = values * cdf
            gelu[:, cols] = gelu_out
            slope[:, cols] = cdf + values * jnp.exp(-0.5 * values * values) * inv_root_two_pi
            sums[0:1, cols] = jnp.sum(gelu_out * gelu_out, axis=0, keepdims=True)
            sums[1:2, cols] = jnp.sum(upstream * gelu_out, axis=0, keepdims=True)
            shift[0:1, cols] = jnp.sum(upstream, axis=0, keepdims=True)


def gradient(sums, other, shift, gain, out_grad, gelu, slope, wide, pre_grad, keep, cross, *scratch):
    turned, gains, shifts = scratch
    squares = sums[0:1, :] + other[0:1, :]
    response = sums[1:2, :] + other[1:2, :]
    channel_norm = jnp.sqrt(squares + 1e-06)
    norm_mean = jnp.sum(channel_norm, axis=1, keepdims=True) * (1.0 / H) + 1e-06
    scaled = channel_norm / norm_mean
    scaled_grad = gain[...] * response
    norm_grad = scaled_grad / norm_mean - jnp.sum(scaled_grad * channel_norm, axis=1, keepdims=True) / (
        H * norm_mean * norm_mean
    )
    of_upstream = gain[...] * scaled + 1.0
    of_gelu = norm_grad / channel_norm
    gain_term = sums[1:2, :] * scaled
    shift_term = shift[...]
    for k in range(H // LANES):
        cols = slice(k * LANES, (k + 1) * LANES)
        upstream = out_grad[:, cols].astype(jnp.float32)
        act_grad = upstream * of_upstream[:, cols] + gelu[:, cols] * of_gelu[:, cols]
        rounded = (act_grad * slope[:, cols]).astype(jnp.bfloat16)
        pre_grad[:, cols] = rounded
        turned[cols, :] = rounded.astype(jnp.float32).T
    both = jnp.concatenate([gain_term, shift_term, jnp.zeros((6, H), jnp.float32)], axis=0)
    for b in range(H // BLOCK):
        tile, start = divmod(b * BLOCK, LANES)
        window = both[:, tile * LANES : min((tile + 2) * LANES, H)]
        if start:
            window = pltpu.roll(window, window.shape[1] - start, 1)
        gains[b : b + 1, :] = window[0:1, :LANES]
        shifts[b : b + 1, :] = window[1:2, :LANES]
    core, x = lax.axis_index("core"), lax.axis_index("x")
    y = 2 * lax.axis_index("yh") + lax.axis_index("yl")
    for of_other in range(2):
        to = core if of_other == 0 else 1 - core
        mine, beside_mine = jnp.where(to == 0, x, y), jnp.where(to == 0, y, x)
        for j in range(4):
            chunk, top = (cross if of_other else keep), j * PART
            d = lax.rem(mine + j, 4)
            for i in range(4):
                e = lax.rem(beside_mine + i, 4)
                block_x, block_y = jnp.where(to == 0, d, e), jnp.where(to == 0, e, d)
                b = (block_y // 2) * 16 + to * 8 + block_x * 2 + lax.rem(block_y, 2)
                start = pl.multiple_of(b * BLOCK, 8)
                units = turned[pl.ds(start, BLOCK), :]
                part = 0 if i in STEPS[0] else 1
                row = top + part * FIRST + STEPS[part].index(i) * BLOCK
                chunk[row : row + BLOCK, :] = units
                row = top + FIRST - 8 + i
                chunk[row : row + 1, :] = gains[pl.ds(b, 1), :]
                chunk[row + 4 : row + 5, :] = shifts[pl.ds(b, 1), :]
    cross[4 * PART :, :] = wide[...]


def store(value, result, sems):
    parts = sems.shape[0]
    rows = ROWS // parts
    copies = [
        pltpu.make_async_copy(value.at[pl.ds(p * rows, rows)], result.at[pl.ds(p * rows, rows)], sems.at[p])
        for p in range(parts)
    ]
    for copy in copies:
        copy.start()
    for copy in copies:
        copy.wait()


def merge(keep, arrived, *outs):
    for j in range(4):
        first, second = outs[j], outs[4 + j]
        for n, source in enumerate((keep, arrived)):
            middle = j * PART + FIRST
            first[n * FIRST : (n + 1) * FIRST, :] = source[j * PART : middle, :]
            second[n * SECOND : (n + 1) * SECOND, :] = source[middle : middle + SECOND, :]


def product(half, blocks, steps, here, *refs):
    arrived = dict(zip(steps, refs[:3]))
    above, below, opposite = arrived[1], arrived[-1], arrived[2]
    (right_first, right_second, right_rest), rest = refs[3:6], refs[6:]
    first = half == 0 and blocks[0] == STEPS[0][0]
    count, height = len(blocks), len(blocks) * BLOCK
    if first:
        outs, terms, lefts = rest[:count], rest[count], rest[count + 1 :]
    else:
        terms, outs, lefts = rest[0], rest[1 : count + 1], rest[count + 1 :]
    step = FIRST if half == 0 else SECOND
    top = STEPS[half].index(blocks[0]) * BLOCK
    one, two = slice(top, top + height), slice(step + top, step + top + height)
    sources = (
        (here[one, :], above[one, :], below[two, :]),
        (above[two, :], below[one, :]),
        (here[two, :], opposite[one, :], opposite[two, :]),
    )
    for left, values in zip(lefts, sources):
        for s, value in enumerate(values):
            below_it = jnp.zeros((left.shape[0] - height, ROWS), jnp.float32)
            value = jnp.concatenate([value, below_it], axis=0) if below_it.size else value
            left[:, s * ROWS : (s + 1) * ROWS] = value.astype(jnp.bfloat16)
    rights = (right_first, right_second, right_rest)
    across_pixels = (((1,), (1,)), ((), ()))
    if first:
        small = jnp.zeros((8, LANES), jnp.float32)
        for pair in (here, above, below, opposite):
            small = small + (pair[FIRST - 8 : FIRST, :] + pair[2 * FIRST - 8 :, :])
        terms[...] = small
    else:
        small = terms[...]
    bias = 0.0
    for left in lefts:
        ones = jnp.ones((8, left.shape[1]), jnp.bfloat16)
        bias = bias + lax.dot_general(ones, left[...], across_pixels, preferred_element_type=jnp.float32)
    width = (height // LANES + 2) * LANES
    bias = jnp.concatenate([bias, jnp.zeros((8, width - bias.shape[1]), jnp.float32)], axis=1)
    rows = []
    for n in range(count):
        tile, start = divmod(n * BLOCK, LANES)
        window = bias[:, tile * LANES : (tile + 2) * LANES]
        rows.append((pltpu.roll(window, 2 * LANES - start, 1) if start else window)[0:1, :LANES])
    small = jnp.concatenate([small, *rows, *[rows[0]] * (8 - count)], axis=0)
    for z in range(8):
        turned = pltpu.roll(small, LANES - z * OWN, 1) if z else small
        for n, (i, out) in enumerate(zip(blocks, outs)):
            row = z * PACKED + 61
            out[row : row + 1, :] = turned[8 + n : 9 + n, :]
            out[row + 1 : row + 2, :] = turned[i : i + 1, :]
            out[row + 2 : row + 3, :] = turned[4 + i : 5 + i, :]
    for group in range(3):
        cols = slice(2 * group * LANES, min(2 * (group + 1) * LANES, C))
        total = 0.0
        for left, right in zip(lefts, rights):
            total = total + lax.dot_general(
                left[...], right[:, cols], (((1,), (0,)), ((), ())), preferred_element_type=jnp.float32
            )
        if group == 2:
            last = total[:, LANES:]
            last = jnp.concatenate([last, last], axis=1)
            last = jnp.concatenate([last, jnp.zeros((8, LANES), jnp.float32)], axis=0)
            left_half = lax.broadcasted_iota(jnp.int32, (6, LANES), 1) < 64
        for n, out in enumerate(outs):
            for z in range(8):
                unit = n * BLOCK + z * OWN
                for k in range(2 * group, min(2 * group + 2, 5)):
                    row, col = z * PACKED + k * OWN, (k - 2 * group) * LANES
                    out[row : row + OWN, :] = total[unit : unit + OWN, col : col + LANES]
                if group == 2:
                    row = z * PACKED + 5 * OWN
                    out[row : row + 6, :] = jnp.where(left_half, last[unit : unit + 6], last[unit + 6 : unit + 12])


PACKED = 64


def add(*refs):
    *parts, out = refs
    total = parts[0][...]
    for part in parts[1:]:
        total = total + part[...]
    out[...] = total


def finish(parts, weight, gain, shift, bias):
    total = parts[0]
    for z in range(1, 8):
        total = total + parts[z]
    for k in range(5):
        weight[:, k * LANES : (k + 1) * LANES] = total[k * OWN : (k + 1) * OWN, :]
    last = total[5 * OWN : 5 * OWN + 6, :]
    weight[:6, 5 * LANES :] = last[:, :64]
    weight[6:, 5 * LANES :] = last[:5, 64:]
    bias[...] = total[61:62, :OWN]
    gain[...] = total[62:63, :OWN]
    shift[...] = total[63:64, :OWN]


def on_device(normed, pre_gelu, out_grad, grn_gain):
    bf16 = jnp.bfloat16
    normed, pre_gelu, out_grad = (
        pltpu.with_memory_space_constraint(v, pltpu.HBM) for v in (normed.T, pre_gelu, out_grad)
    )
    wide = call(
        widen,
        f32(C, ROWS),
        scratch=[pltpu.VMEM((C, ROWS), bf16), pltpu.SemaphoreType.DMA((2,))],
        moved=540_000,
        in_specs=[pl.BlockSpec(memory_space=pl.ANY)],
    )(normed)
    sums, shift, gelu, slope, upstream = call(
        statistics,
        [f32(2, H), f32(1, H), f32(ROWS, H), f32(ROWS, H), jax.ShapeDtypeStruct((ROWS, H), bf16)],
        scratch=[pltpu.VMEM((ROWS, H), bf16), pltpu.SemaphoreType.DMA((2, 4))],
        flops=0,
        moved=4_400_000,
        in_specs=[pl.BlockSpec(memory_space=pl.ANY)] * 2,
    )(pre_gelu, out_grad)
    other = send(sums, other_half)

    from_below = send(wide, along(1))
    from_above = send(wide, along(-1))
    below_across = send(wide, across(1))
    above_across = send(wide, across(-1))

    def right_of(*wides, flops=GUIDE):
        shape = jax.ShapeDtypeStruct((len(wides) * ROWS, C), bf16)
        return call(narrow, shape, flops=flops, moved=4_400_000)(*wides)

    pre_grad, keep, cross = call(
        gradient,
        [jax.ShapeDtypeStruct((ROWS, H), bf16), f32(4 * PART, LANES), f32(4 * PART + C, LANES)],
        scratch=[
            pltpu.VMEM((H, LANES), jnp.float32),
            pltpu.VMEM((H // BLOCK, LANES), jnp.float32),
            pltpu.VMEM((H // BLOCK, LANES), jnp.float32),
        ],
        flops=0,
        moved=6_000_000,
    )(sums, other, shift, grn_gain.reshape(1, H), upstream, gelu, slope, wide)
    arrived = send(cross, other_core)
    right_first = right_of(wide, from_below, above_across, flops=GUIDE)
    arrived, right_first = lax.optimization_barrier((arrived, right_first))
    firsts_and_seconds = call(
        merge, [f32(2 * FIRST, LANES)] * 4 + [f32(2 * SECOND, LANES)] * 4, moved=4_400_000
    )(keep, arrived)
    far = send(from_below, along(1))
    far_across = send(above_across, along(-1))
    firsts, seconds = list(firsts_and_seconds[:4]), list(firsts_and_seconds[4:])
    firsts[1], below_across, from_above = lax.optimization_barrier((firsts[1], below_across, from_above))
    right_second = right_of(below_across, from_above, flops=GUIDE)
    right_rest = right_of(arrived, far, far_across, flops=GUIDE)

    def around(steps, own, *away):
        return own, *(send(away[(step - 1) % 4], along(step)) for step in steps)

    def multiply(half, blocks, steps, parts, terms=(), flops=0):
        count = len(blocks)
        outs = [f32(8 * PACKED, LANES)] * count + ([] if terms else [f32(8, LANES)])
        height = (count * BLOCK + 15) // 16 * 16
        return call(
            functools.partial(product, half, blocks, steps),
            outs,
            scratch=[pltpu.VMEM((height, n * ROWS), bf16) for n in (3, 2, 3)],
            flops=flops,
            moved=4_000_000,
        )(*parts, right_first, right_second, right_rest, *terms)

    def reduce_beside(half, products):
        return [value if i == 0 else send(value, beside(-1 if i == 3 else i)) for i, value in zip(STEPS[half], products)]

    def add_up(*values, flops=0):
        return call(add, f32(8 * PACKED, LANES), flops=flops, moved=700_000)(*values)

    steps = (1, -1, 2)
    parts = around(steps, *firsts)
    one, terms = multiply(0, STEPS[0][:1], steps, parts, flops=GUIDE)
    products = [one, *multiply(0, STEPS[0][1:], steps, parts, (terms,), flops=GUIDE)]
    rows = add_up(*reduce_beside(0, products), flops=GUIDE // 10)
    rows, pre_grad = lax.optimization_barrier((rows, pre_grad))
    pre_grad = call(
        store,
        jax.ShapeDtypeStruct((ROWS, H), bf16),
        scratch=[pltpu.SemaphoreType.DMA((4,))],
        moved=1_440_000,
        in_specs=[pl.BlockSpec(memory_space=pltpu.VMEM)],
        out_specs=pl.BlockSpec(memory_space=pl.ANY),
    )(pre_grad)
    rows, pre_grad = lax.optimization_barrier((rows, pre_grad))
    parts = around(steps, *seconds)
    others = multiply(1, STEPS[1][:1], steps, parts, (terms,), flops=GUIDE)
    others = [*others, *multiply(1, STEPS[1][1:], steps, parts, (terms,), flops=0)]
    rows = add_up(rows, *reduce_beside(1, others))
    rows = lax.all_to_all(rows.reshape(8, PACKED, LANES), "z", 0, 0, tiled=True)
    weight, gain, shift, bias = call(
        finish, [f32(OWN, C), f32(1, OWN), f32(1, OWN), f32(1, OWN)], moved=330_000
    )(rows)
    return pre_grad, weight, gain.reshape(OWN), shift.reshape(OWN), bias.reshape(OWN)


def solution(mesh):
    split = Mesh(mesh.devices.reshape(SIZES), AXES)
    return jax.shard_map(
        on_device,
        mesh=split,
        in_specs=(P(AXES, None), P(AXES, None), P(AXES, None), P()),
        out_specs=(P(AXES, None), P(AXES, None), P(AXES), P(AXES), P(AXES)),
        check_vma=False,
    )
```

```python
import functools

import jax
import jax.numpy as jnp
import numpy as np
from jax import lax
from jax.experimental import pallas as pl
from jax.experimental.pallas import tpu as pltpu
from jax.sharding import Mesh, PartitionSpec as P

root_half = 0.7071067811865476
inv_root_two_pi = 0.3989422804014327

AXES = ("yh", "core", "x", "yl", "z")
SIZES = (2, 2, 4, 2, 8)
ROWS = 128
C = 704
H = 2816
BLOCK = 88
OWN = 11
STEPS = ((1, 2), (3, 0))
FIRST = len(STEPS[0]) * BLOCK + 8
SECOND = len(STEPS[1]) * BLOCK
PART = FIRST + SECOND
LANES = 128
MIB = 1 << 20
GUIDE = 20_000_000_000


def pairs(target):
    found = []
    for i in range(256):
        yh, core, x, yl, z = (int(v) for v in np.unravel_index(i, SIZES))
        core2, x2, y2, z2 = target(core, x, 2 * yh + yl, z)
        place = (y2 // 2 % 2, core2 % 2, x2 % 4, y2 % 2, z2 % 8)
        found.append((i, int(np.ravel_multi_index(place, SIZES))))
    return found


def send(value, target):
    return lax.ppermute(value, AXES, pairs(target))


def other_core(core, x, y, z):
    return 1 - core, x, y, z


def other_half(core, x, y, z):
    return core, x, y, z ^ 1


def along(k):
    return lambda core, x, y, z: (core, x + k, y, z) if core == 0 else (core, x, y + k, z)


def across(k):
    return lambda core, x, y, z: (1, x, y + k, z) if core == 0 else (0, x + k, y, z)


def beside(k):
    return lambda core, x, y, z: (core, x, y + k, z) if core == 0 else (core, x + k, y, z)


def call(body, out_shape, scratch=(), flops=0, moved=0, limit=24, **specs):
    return pl.pallas_call(
        body,
        out_shape=out_shape,
        **specs,
        scratch_shapes=scratch,
        compiler_params=pltpu.CompilerParams(vmem_limit_bytes=limit * MIB),
        cost_estimate=pl.CostEstimate(flops=flops, bytes_accessed=moved, transcendentals=0),
    )


def f32(*shape):
    return jax.ShapeDtypeStruct(shape, jnp.float32)


def narrow(*refs):
    *wides, out = refs
    for s, wide in enumerate(wides):
        top = wide.shape[0] - C
        out[s * ROWS : (s + 1) * ROWS, :] = wide[top:, :].T.astype(jnp.bfloat16)


CUTS = (0, 6, 12, 17, 22)


def widen(normed_hbm, wide, normed, sems):
    half = C // 2
    copies = [
        pltpu.make_async_copy(normed_hbm.at[pl.ds(p * half, half)], normed.at[pl.ds(p * half, half)], sems.at[p])
        for p in range(2)
    ]
    for copy in copies:
        copy.start()
    for p, copy in enumerate(copies):
        copy.wait()
        rows = slice(p * half, (p + 1) * half)
        wide[rows, :] = normed[rows, :].astype(jnp.float32)


def statistics(pre_gelu_hbm, out_grad_hbm, sums, shift, gelu, slope, out_grad, pre_gelu, sems):
    copies = []
    for p, (start, stop) in enumerate(zip(CUTS[:-1], CUTS[1:])):
        cols = pl.ds(start * LANES, (stop - start) * LANES)
        for n, (source, target) in enumerate(((pre_gelu_hbm, pre_gelu), (out_grad_hbm, out_grad))):
            copies.append(pltpu.make_async_copy(source.at[:, cols], target.at[:, cols], sems.at[n, p]))
            copies[-1].start()
    for p, (start, stop) in enumerate(zip(CUTS[:-1], CUTS[1:])):
        copies[2 * p].wait()
        copies[2 * p + 1].wait()
        for k in range(start, stop):
            cols = slice(k * LANES, (k + 1) * LANES)
            values = pre_gelu[:, cols].astype(jnp.float32)
            upstream = out_grad[:, cols].astype(jnp.float32)
            cdf = 0.5 * (1.0 + lax.erf(values * root_half))
            gelu_out = values * cdf
            gelu[:, cols] = gelu_out
            slope[:, cols] = cdf + values * jnp.exp(-0.5 * values * values) * inv_root_two_pi
            sums[0:1, cols] = jnp.sum(gelu_out * gelu_out, axis=0, keepdims=True)
            sums[1:2, cols] = jnp.sum(upstream * gelu_out, axis=0, keepdims=True)
            shift[0:1, cols] = jnp.sum(upstream, axis=0, keepdims=True)


def gradient(sums, other, shift, gain, out_grad, gelu, slope, wide, pre_grad, keep, cross, *scratch):
    turned, gains, shifts = scratch
    squares = sums[0:1, :] + other[0:1, :]
    response = sums[1:2, :] + other[1:2, :]
    channel_norm = jnp.sqrt(squares + 1e-06)
    norm_mean = jnp.sum(channel_norm, axis=1, keepdims=True) * (1.0 / H) + 1e-06
    scaled = channel_norm / norm_mean
    scaled_grad = gain[...] * response
    norm_grad = scaled_grad / norm_mean - jnp.sum(scaled_grad * channel_norm, axis=1, keepdims=True) / (
        H * norm_mean * norm_mean
    )
    of_upstream = gain[...] * scaled + 1.0
    of_gelu = norm_grad / channel_norm
    gain_term = sums[1:2, :] * scaled
    shift_term = shift[...]
    for k in range(H // LANES):
        cols = slice(k * LANES, (k + 1) * LANES)
        upstream = out_grad[:, cols].astype(jnp.float32)
        act_grad = upstream * of_upstream[:, cols] + gelu[:, cols] * of_gelu[:, cols]
        rounded = (act_grad * slope[:, cols]).astype(jnp.bfloat16)
        pre_grad[:, cols] = rounded
        turned[cols, :] = rounded.astype(jnp.float32).T
    both = jnp.concatenate([gain_term, shift_term, jnp.zeros((6, H), jnp.float32)], axis=0)
    for b in range(H // BLOCK):
        tile, start = divmod(b * BLOCK, LANES)
        window = both[:, tile * LANES : min((tile + 2) * LANES, H)]
        if start:
            window = pltpu.roll(window, window.shape[1] - start, 1)
        gains[b : b + 1, :] = window[0:1, :LANES]
        shifts[b : b + 1, :] = window[1:2, :LANES]
    core, x = lax.axis_index("core"), lax.axis_index("x")
    y = 2 * lax.axis_index("yh") + lax.axis_index("yl")
    for of_other in range(2):
        to = core if of_other == 0 else 1 - core
        mine, beside_mine = jnp.where(to == 0, x, y), jnp.where(to == 0, y, x)
        for j in range(4):
            chunk, top = (cross if of_other else keep), j * PART
            d = lax.rem(mine + j, 4)
            for i in range(4):
                e = lax.rem(beside_mine + i, 4)
                block_x, block_y = jnp.where(to == 0, d, e), jnp.where(to == 0, e, d)
                b = (block_y // 2) * 16 + to * 8 + block_x * 2 + lax.rem(block_y, 2)
                start = pl.multiple_of(b * BLOCK, 8)
                units = turned[pl.ds(start, BLOCK), :]
                part = 0 if i in STEPS[0] else 1
                row = top + part * FIRST + STEPS[part].index(i) * BLOCK
                chunk[row : row + BLOCK, :] = units
                row = top + FIRST - 8 + i
                chunk[row : row + 1, :] = gains[pl.ds(b, 1), :]
                chunk[row + 4 : row + 5, :] = shifts[pl.ds(b, 1), :]
    cross[4 * PART :, :] = wide[...]


def store(value, result, sems):
    parts = sems.shape[0]
    rows = ROWS // parts
    copies = [
        pltpu.make_async_copy(value.at[pl.ds(p * rows, rows)], result.at[pl.ds(p * rows, rows)], sems.at[p])
        for p in range(parts)
    ]
    for copy in copies:
        copy.start()
    for copy in copies:
        copy.wait()


def merge(keep, arrived, *outs):
    for j in range(4):
        first, second = outs[j], outs[4 + j]
        for n, source in enumerate((keep, arrived)):
            middle = j * PART + FIRST
            first[n * FIRST : (n + 1) * FIRST, :] = source[j * PART : middle, :]
            second[n * SECOND : (n + 1) * SECOND, :] = source[middle : middle + SECOND, :]


def product(half, blocks, steps, here, *refs):
    arrived = dict(zip(steps, refs[:3]))
    above, below, opposite = arrived[1], arrived[-1], arrived[2]
    (right_first, right_second, right_rest), rest = refs[3:6], refs[6:]
    first = half == 0 and blocks[0] == STEPS[0][0]
    count, height = len(blocks), len(blocks) * BLOCK
    if first:
        outs, terms, lefts = rest[:count], rest[count], rest[count + 1 :]
    else:
        terms, outs, lefts = rest[0], rest[1 : count + 1], rest[count + 1 :]
    step = FIRST if half == 0 else SECOND
    top = STEPS[half].index(blocks[0]) * BLOCK
    one, two = slice(top, top + height), slice(step + top, step + top + height)
    sources = (
        (here[one, :], above[one, :], below[two, :]),
        (above[two, :], below[one, :]),
        (here[two, :], opposite[one, :], opposite[two, :]),
    )
    for left, values in zip(lefts, sources):
        for s, value in enumerate(values):
            below_it = jnp.zeros((left.shape[0] - height, ROWS), jnp.float32)
            value = jnp.concatenate([value, below_it], axis=0) if below_it.size else value
            left[:, s * ROWS : (s + 1) * ROWS] = value.astype(jnp.bfloat16)
    rights = (right_first, right_second, right_rest)
    across_pixels = (((1,), (1,)), ((), ()))
    if first:
        small = jnp.zeros((8, LANES), jnp.float32)
        for pair in (here, above, below, opposite):
            small = small + (pair[FIRST - 8 : FIRST, :] + pair[2 * FIRST - 8 :, :])
        terms[...] = small
    else:
        small = terms[...]
    bias = 0.0
    for left in lefts:
        ones = jnp.ones((8, left.shape[1]), jnp.bfloat16)
        bias = bias + lax.dot_general(ones, left[...], across_pixels, preferred_element_type=jnp.float32)
    width = (height // LANES + 2) * LANES
    bias = jnp.concatenate([bias, jnp.zeros((8, width - bias.shape[1]), jnp.float32)], axis=1)
    rows = []
    for n in range(count):
        tile, start = divmod(n * BLOCK, LANES)
        window = bias[:, tile * LANES : (tile + 2) * LANES]
        rows.append((pltpu.roll(window, 2 * LANES - start, 1) if start else window)[0:1, :LANES])
    small = jnp.concatenate([small, *rows, *[rows[0]] * (8 - count)], axis=0)
    for z in range(8):
        turned = pltpu.roll(small, LANES - z * OWN, 1) if z else small
        for n, (i, out) in enumerate(zip(blocks, outs)):
            row = z * PACKED + 61
            out[row : row + 1, :] = turned[8 + n : 9 + n, :]
            out[row + 1 : row + 2, :] = turned[i : i + 1, :]
            out[row + 2 : row + 3, :] = turned[4 + i : 5 + i, :]
    for group in range(3):
        cols = slice(2 * group * LANES, min(2 * (group + 1) * LANES, C))
        total = 0.0
        for left, right in zip(lefts, rights):
            total = total + lax.dot_general(
                left[...], right[:, cols], (((1,), (0,)), ((), ())), preferred_element_type=jnp.float32
            )
        if group == 2:
            last = total[:, LANES:]
            last = jnp.concatenate([last, last], axis=1)
            last = jnp.concatenate([last, jnp.zeros((8, LANES), jnp.float32)], axis=0)
            left_half = lax.broadcasted_iota(jnp.int32, (6, LANES), 1) < 64
        for n, out in enumerate(outs):
            for z in range(8):
                unit = n * BLOCK + z * OWN
                for k in range(2 * group, min(2 * group + 2, 5)):
                    row, col = z * PACKED + k * OWN, (k - 2 * group) * LANES
                    out[row : row + OWN, :] = total[unit : unit + OWN, col : col + LANES]
                if group == 2:
                    row = z * PACKED + 5 * OWN
                    out[row : row + 6, :] = jnp.where(left_half, last[unit : unit + 6], last[unit + 6 : unit + 12])


PACKED = 64


def add(*refs):
    *parts, out = refs
    total = parts[0][...]
    for part in parts[1:]:
        total = total + part[...]
    out[...] = total


def finish(parts, weight, gain, shift, bias):
    total = parts[0]
    for z in range(1, 8):
        total = total + parts[z]
    for k in range(5):
        weight[:, k * LANES : (k + 1) * LANES] = total[k * OWN : (k + 1) * OWN, :]
    last = total[5 * OWN : 5 * OWN + 6, :]
    weight[:6, 5 * LANES :] = last[:, :64]
    weight[6:, 5 * LANES :] = last[:5, 64:]
    bias[...] = total[61:62, :OWN]
    gain[...] = total[62:63, :OWN]
    shift[...] = total[63:64, :OWN]


def on_device(normed, pre_gelu, out_grad, grn_gain):
    bf16 = jnp.bfloat16
    normed, pre_gelu, out_grad = (
        pltpu.with_memory_space_constraint(v, pltpu.HBM) for v in (normed.T, pre_gelu, out_grad)
    )
    wide = call(
        widen,
        f32(C, ROWS),
        scratch=[pltpu.VMEM((C, ROWS), bf16), pltpu.SemaphoreType.DMA((2,))],
        moved=540_000,
        in_specs=[pl.BlockSpec(memory_space=pl.ANY)],
    )(normed)
    sums, shift, gelu, slope, upstream = call(
        statistics,
        [f32(2, H), f32(1, H), f32(ROWS, H), f32(ROWS, H), jax.ShapeDtypeStruct((ROWS, H), bf16)],
        scratch=[pltpu.VMEM((ROWS, H), bf16), pltpu.SemaphoreType.DMA((2, 4))],
        flops=0,
        moved=4_400_000,
        in_specs=[pl.BlockSpec(memory_space=pl.ANY)] * 2,
    )(pre_gelu, out_grad)
    other = send(sums, other_half)

    from_below = send(wide, along(1))
    from_above = send(wide, along(-1))
    below_across = send(wide, across(1))
    above_across = send(wide, across(-1))

    def right_of(*wides, flops=GUIDE):
        shape = jax.ShapeDtypeStruct((len(wides) * ROWS, C), bf16)
        return call(narrow, shape, flops=flops, moved=4_400_000)(*wides)

    pre_grad, keep, cross = call(
        gradient,
        [jax.ShapeDtypeStruct((ROWS, H), bf16), f32(4 * PART, LANES), f32(4 * PART + C, LANES)],
        scratch=[
            pltpu.VMEM((H, LANES), jnp.float32),
            pltpu.VMEM((H // BLOCK, LANES), jnp.float32),
            pltpu.VMEM((H // BLOCK, LANES), jnp.float32),
        ],
        flops=0,
        moved=6_000_000,
    )(sums, other, shift, grn_gain.reshape(1, H), upstream, gelu, slope, wide)
    arrived = send(cross, other_core)
    right_first = right_of(wide, from_below, above_across, flops=GUIDE)
    arrived, right_first = lax.optimization_barrier((arrived, right_first))
    firsts_and_seconds = call(
        merge, [f32(2 * FIRST, LANES)] * 4 + [f32(2 * SECOND, LANES)] * 4, moved=4_400_000
    )(keep, arrived)
    far = send(from_below, along(1))
    far_across = send(above_across, along(-1))
    firsts, seconds = list(firsts_and_seconds[:4]), list(firsts_and_seconds[4:])
    firsts[3], below_across, from_above = lax.optimization_barrier((firsts[3], below_across, from_above))
    right_second = right_of(below_across, from_above, flops=GUIDE)
    right_rest = right_of(arrived, far, far_across, flops=GUIDE)

    def around(steps, own, *away):
        return own, *(send(away[(step - 1) % 4], along(step)) for step in steps)

    def multiply(half, blocks, steps, parts, terms=(), flops=0):
        count = len(blocks)
        outs = [f32(8 * PACKED, LANES)] * count + ([] if terms else [f32(8, LANES)])
        height = (count * BLOCK + 15) // 16 * 16
        return call(
            functools.partial(product, half, blocks, steps),
            outs,
            scratch=[pltpu.VMEM((height, n * ROWS), bf16) for n in (3, 2, 3)],
            flops=flops,
            moved=4_000_000,
        )(*parts, right_first, right_second, right_rest, *terms)

    def reduce_beside(half, products):
        return [value if i == 0 else send(value, beside(-1 if i == 3 else i)) for i, value in zip(STEPS[half], products)]

    def add_up(*values, flops=0):
        return call(add, f32(8 * PACKED, LANES), flops=flops, moved=700_000)(*values)

    steps = (1, -1, 2)
    parts = around(steps, *firsts)
    one, terms = multiply(0, STEPS[0][:1], steps, parts, flops=GUIDE)
    products = [one, *multiply(0, STEPS[0][1:], steps, parts, (terms,), flops=GUIDE)]
    rows = add_up(*reduce_beside(0, products), flops=GUIDE // 10)
    rows, pre_grad = lax.optimization_barrier((rows, pre_grad))
    pre_grad = call(
        store,
        jax.ShapeDtypeStruct((ROWS, H), bf16),
        scratch=[pltpu.SemaphoreType.DMA((4,))],
        moved=1_440_000,
        in_specs=[pl.BlockSpec(memory_space=pltpu.VMEM)],
        out_specs=pl.BlockSpec(memory_space=pl.ANY),
    )(pre_grad)
    rows, pre_grad = lax.optimization_barrier((rows, pre_grad))
    parts = around(steps, *seconds)
    others = multiply(1, STEPS[1][:1], steps, parts, (terms,), flops=GUIDE)
    others = [*others, *multiply(1, STEPS[1][1:], steps, parts, (terms,), flops=0)]
    rows = add_up(rows, *reduce_beside(1, others))
    rows = lax.all_to_all(rows.reshape(8, PACKED, LANES), "z", 0, 0, tiled=True)
    weight, gain, shift, bias = call(
        finish, [f32(OWN, C), f32(1, OWN), f32(1, OWN), f32(1, OWN)], moved=330_000
    )(rows)
    return pre_grad, weight, gain.reshape(OWN), shift.reshape(OWN), bias.reshape(OWN)


def solution(mesh):
    split = Mesh(mesh.devices.reshape(SIZES), AXES)
    return jax.shard_map(
        on_device,
        mesh=split,
        in_specs=(P(AXES, None), P(AXES, None), P(AXES, None), P()),
        out_specs=(P(AXES, None), P(AXES, None), P(AXES), P(AXES), P(AXES)),
        check_vma=False,
    )
```
